32 devices in a mesh: grp: 2 (over y), gx: 4 (over x, core), gy: 4 (over z).
Axes of the slice: x: 2, y: 2, z: 4, core: 2. Of those that a mesh axis runs over, the one named last changes fastest.
Arguments:
- hidden: bfloat16 [1536, 14336], P(('grp', 'gy'), 'gx'), parts along dimension 0, may hold values from -6 to 6
- parents: int32 [1536], P('grp'), parts along dimension 0, may hold values from 0 to 767, as said below
- depth_table: bfloat16 [256, 14336], P(None, 'gx'), may hold values from -6 to 6
- weight: bfloat16 [14336, 36864], P('gx', 'gy'), may hold values from -0.046875 to 0.046875
Outputs:
- activated: bfloat16 [1536, 36864], P(('grp', 'gx'), 'gy'), parts along dimension 0
The draws below stay inside these ranges and needn't reach their ends.
There are 2 independent parts, one for each index of `grp`. The reference program is written for one: setup_inputs(seed, part) draws one part's arguments, and reference() takes and returns one part's arrays. A program takes and returns all parts, laid end to end along the dimension named above; an argument that names none is the same for every part. Nothing has to cross between parts.
Inputs may be any that keep to these rules, and one draw needn't show every extreme that they name: `parents`: rows come in 3 trees of 256 rows; the first row of each tree is its root and names itself; every other row names an earlier row of its own tree.
All inputs are finite; a program needn't handle non-finite values.
Results may differ from the reference program's by a relative error of at most 0.012.
Values may be sent and summed in bfloat16 or wider, within the bound.
No kernel may reach another device: no remote copies, remote signals or barrier semaphores. Data moves between devices by JAX's collectives and lax.ppermute only.
A program may use at most 192 MiB of HBM per device.

```python
import jax
import jax.numpy as jnp
from jax import lax

D = 14336
FF = 36864
TREE = 256
TREES = 3
ROWS = 768
N_GX = 4


def draw_parents(key, part):
    key = jax.random.fold_in(key, 7)
    local = jnp.arange(TREE, dtype=jnp.int32)
    upper = jnp.maximum(local, 1)[None, :]
    raw = jax.random.randint(key, (TREES, TREE), 0, upper)
    offset = (jnp.arange(TREES, dtype=jnp.int32) * TREE)[:, None]
    return (raw + offset).reshape(TREES * TREE).astype(jnp.int32)


def block_scale(rng, dims, cuts, low, largest):
    def one(dim, shards_of):
        heights = jax.random.uniform(jax.random.fold_in(jax.random.fold_in(rng, 6), dim), (shards_of,), jnp.float32, low / len(cuts), largest / len(cuts))
        return jnp.repeat(jnp.exp(heights), dims[dim] // shards_of).reshape((-1,) + (1,) * (len(dims) - dim - 1))

    factor_of = one(*cuts[0])
    for cut in cuts[1:]:
        factor_of = factor_of * one(*cut)
    return factor_of


def normal_values(stream_key, extent, width, most, cuts=(), held_as=jnp.bfloat16):
    array = width * jax.random.normal(stream_key, extent, jnp.float32)
    if cuts:
        array = array * block_scale(stream_key, extent, cuts, -0.22, 0.18)
    return jnp.clip(array, -most, most).astype(held_as)


def setup_inputs(seed: int = 0, part: int = 0) -> dict:
    streams_of = jax.random.split(jax.random.key(seed), 5)
    part_keys = jax.random.split(jax.random.fold_in(streams_of[4], part), 5)
    return {
        "hidden": normal_values(part_keys[0], (ROWS, D), 1.0, 6.0, ((0, 4), (1, 4))),
        "parents": draw_parents(jax.random.fold_in(jax.random.fold_in(streams_of[4], part), 71), part),
        "depth_table": normal_values(streams_of[2], (TREE, D), 1.0, 6.0, ((1, 4),)),
        "weight": normal_values(streams_of[3], (D, FF), D ** -0.5, 0.046875, ((0, 4), (1, 4))),
    }


def tree_depth(parents, steps):
    index = jnp.arange(parents.shape[0], dtype=jnp.int32)
    depth = (parents != index).astype(jnp.int32)
    pointer = parents
    for level in range(steps):
        depth = depth + depth[pointer]
        pointer = pointer[pointer]
    return depth


def reference(hidden, parents, depth_table, weight):
    depth = tree_depth(parents, depth_table.shape[0].bit_length())
    rows_in = (hidden.astype(jnp.float32) + depth_table[depth].astype(jnp.float32)).astype(jnp.bfloat16)
    block = D // N_GX
    total = jnp.zeros((rows_in.shape[0], weight.shape[1]), jnp.float32)
    for part_k in range(N_GX):
        term = jnp.dot(rows_in[:, part_k * block:(part_k + 1) * block], weight[part_k * block:(part_k + 1) * block], preferred_element_type=jnp.float32).astype(jnp.bfloat16)
        term = lax.optimization_barrier(term)
        total = total + term.astype(jnp.float32)
    return jax.nn.gelu(total, approximate=True).astype(jnp.bfloat16)
```

```python
import functools

import jax
import jax.numpy as jnp
from jax import lax
from jax.experimental import pallas as pl
from jax.experimental.pallas import tpu as pltpu
from jax.sharding import PartitionSpec as P

BF16 = jnp.bfloat16
F32 = jnp.float32
MIB = 1024 * 1024


def onehot_kernel(tree, parents_ref, onehot_ref):
    lanes = lax.broadcasted_iota(jnp.int32, (tree, tree), 1)
    rows = lax.broadcasted_iota(jnp.int32, (tree, 1), 0)
    for first in range(0, onehot_ref.shape[0], tree):
        parent = parents_ref[first:first + tree, :] - first
        jump = (parent == lanes).astype(BF16)
        depth = jnp.broadcast_to((parent != rows).astype(F32), (tree, 128))
        for level in range((tree - 1).bit_length()):
            depth = depth + jnp.dot(jump, depth.astype(BF16), preferred_element_type=F32)
            jump = jnp.dot(jump, jump, preferred_element_type=F32).astype(BF16)
        onehot_ref[first:first + tree, :] = (depth[:, :1].astype(jnp.int32) == lanes).astype(BF16)


def depth_onehot(parents, tree):
    rows = parents.shape[0]
    return pl.pallas_call(
        functools.partial(onehot_kernel, tree),
        out_shape=jax.ShapeDtypeStruct((rows, tree), BF16),
        compiler_params=pltpu.CompilerParams(vmem_limit_bytes=16 * MIB),
        cost_estimate=pl.CostEstimate(flops=48 * rows * tree * tree, bytes_accessed=8 * rows * tree, transcendentals=0),
    )(parents[:, None])


def embed_kernel(n_gx, n_gy, first, size, place_ref, onehot_ref, table_ref, hidden_ref, rows_ref):
    chips = n_gx // 2
    block = onehot_ref.shape[0] // n_gy
    x, core = place_ref[0] // 2, place_ref[0] % 2
    for dest in range(n_gx):
        ahead = lax.rem(dest // 2 - x + 2 * chips - 1, chips)
        slot = jnp.where(core == dest % 2, chips, 0) + ahead
        here = dest * block + first
        looked = jnp.dot(onehot_ref[here:here + size, :], table_ref[...], preferred_element_type=F32)
        total = hidden_ref[dest * size:(dest + 1) * size, :].astype(F32) + looked
        rows_ref[pl.ds(pl.multiple_of(slot * size, size), size), :] = total.astype(BF16)


def embed(n_gx, n_gy, first, size, place, onehot, table, hidden):
    rows, depth = hidden.shape
    vmem = pl.BlockSpec(memory_space=pltpu.VMEM)
    return pl.pallas_call(
        functools.partial(embed_kernel, n_gx, n_gy, first, size),
        out_shape=jax.ShapeDtypeStruct((rows, depth), BF16),
        in_specs=[pl.BlockSpec(memory_space=pltpu.SMEM)] + [vmem] * 3,
        out_specs=vmem,
        compiler_params=pltpu.CompilerParams(vmem_limit_bytes=24 * MIB),
        cost_estimate=pl.CostEstimate(flops=2 * rows * 256 * depth, bytes_accessed=6 * rows * depth, transcendentals=0),
    )(place, onehot, table, hidden)


def product_kernel(rows_ref, weight_ref, out_ref):
    out_ref[...] = jnp.dot(rows_ref[...], weight_ref[...], preferred_element_type=F32).astype(BF16)


def product(rows, weight, start, width, tile):
    height, depth = rows.shape
    return pl.pallas_call(
        product_kernel,
        grid=(width // tile,),
        out_shape=jax.ShapeDtypeStruct((height, width), BF16),
        in_specs=[
            pl.BlockSpec((height, depth), lambda j: (0, 0)),
            pl.BlockSpec((depth, tile), lambda j: (0, start // tile + j)),
        ],
        out_specs=pl.BlockSpec((height, tile), lambda j: (0, j)),
        compiler_params=pltpu.CompilerParams(vmem_limit_bytes=32 * MIB),
        cost_estimate=pl.CostEstimate(
            flops=2 * height * depth * width,
            bytes_accessed=2 * (height * depth + depth * width + height * width),
            transcendentals=0,
        ),
    )(rows, weight)


def row_chunks(block):
    for parts in (4, 3, 2):
        if block % (16 * parts) == 0:
            return [block // parts] * parts
    return [block]


def pieces_of(columns, count):
    while columns % (count * 256):
        count -= 1
    return count


def local(n_gx, n_gy, hidden, parents, depth_table, weight):
    tree = depth_table.shape[0]
    columns = weight.shape[1]
    block = hidden.shape[0]
    chips = n_gx // 2
    place = lax.axis_index("gx").astype(jnp.int32)[None]

    sizes = row_chunks(block)
    gathered, first = [], 0
    for size in sizes:
        gathered.append(lax.all_gather(hidden[first:first + size], "gy", axis=0, tiled=True))
        first += size

    onehot = depth_onehot(parents, tree)
    sibling = [(g, g ^ 1) for g in range(n_gx)]

    def across(ahead):
        return [(g, (g // 2 + ahead) % chips * 2 + g % 2) for g in range(n_gx)]

    parts, first = [], 0
    for index, size in enumerate(sizes):
        rows = embed(n_gx, n_gy, first, size, place, onehot, depth_table, gathered[index])
        first += size
        count = pieces_of(columns, 4 if index == len(sizes) - 1 else 2)
        width = columns // count
        tile = 512 if width % 512 == 0 else 256
        done = []
        for piece in range(count):
            out = product(rows, weight, piece * width, width, tile)
            got = lax.ppermute(out[:chips * size], "gx", sibling)
            pair = (out[chips * size:].astype(F32) + got.astype(F32)).astype(BF16)
            total = pair[(chips - 1) * size:].astype(F32)
            for ahead in range(1, chips):
                total = total + lax.ppermute(pair[(ahead - 1) * size:ahead * size], "gx", across(ahead)).astype(F32)
            done.append(jax.nn.gelu(total, approximate=True).astype(BF16))
        parts.append(jnp.concatenate(done, axis=1))
    return jnp.concatenate(parts, axis=0)


def solution(mesh):
    return jax.shard_map(
        functools.partial(local, mesh.shape["gx"], mesh.shape["gy"]),
        mesh=mesh,
        in_specs=(P(("grp", "gy"), "gx"), P("grp"), P(None, "gx"), P("gx", "gy")),
        out_specs=P(("grp", "gx"), "gy"),
        check_vma=False,
    )
```

```python
import functools

import jax
import jax.numpy as jnp
from jax import lax
from jax.experimental import pallas as pl
from jax.experimental.pallas import tpu as pltpu
from jax.sharding import PartitionSpec as P

BF16 = jnp.bfloat16
F32 = jnp.float32
MIB = 1024 * 1024
ANY = pl.BlockSpec(memory_space=pl.ANY)
VMEM = pl.BlockSpec(memory_space=pltpu.VMEM)
SMEM = pl.BlockSpec(memory_space=pltpu.SMEM)


def params(limit):
    return pltpu.CompilerParams(vmem_limit_bytes=limit * MIB)


def cost(flops, accessed):
    return pl.CostEstimate(flops=8 * flops, bytes_accessed=8 * accessed, transcendentals=0)


def divisor(extent, choices):
    for choice in choices:
        if extent % choice == 0:
            return choice
    return extent


def onehot_kernel(tree, parents_ref, onehot_ref):
    lanes = lax.broadcasted_iota(jnp.int32, (tree, tree), 1)
    rows = lax.broadcasted_iota(jnp.int32, (tree, 1), 0)
    for first in range(0, onehot_ref.shape[0], tree):
        parent = parents_ref[first:first + tree, :] - first
        jump = (parent == lanes).astype(BF16)
        depth = jnp.broadcast_to((parent != rows).astype(F32), (tree, 128))
        for level in range((tree - 1).bit_length()):
            depth = depth + jnp.dot(jump, depth.astype(BF16), preferred_element_type=F32)
            jump = jnp.dot(jump, jump, preferred_element_type=F32).astype(BF16)
        onehot_ref[first:first + tree, :] = (depth[:, :1].astype(jnp.int32) == lanes).astype(BF16)


def depth_onehot(parents, tree):
    rows = parents.shape[0]
    return pl.pallas_call(
        functools.partial(onehot_kernel, tree),
        name="onehot",
        out_shape=jax.ShapeDtypeStruct((rows, tree), BF16),
        compiler_params=params(16),
        cost_estimate=cost(48 * rows * tree * tree, 8 * rows * tree),
    )(parents[:, None])


def forward_kernel(place_ref, near_ref, far_ref, *refs):
    out_ref = refs[-1]
    outer = jnp.logical_or(place_ref[1] == 0, place_ref[1] == 3)

    @pl.when(outer)
    def _():
        out_ref[...] = near_ref[...]

    @pl.when(jnp.logical_not(outer))
    def _():
        out_ref[...] = far_ref[...]


def forward(place, near, far, after):
    return pl.pallas_call(
        forward_kernel,
        name="forward",
        out_shape=jax.ShapeDtypeStruct(near.shape, near.dtype),
        in_specs=[SMEM, VMEM, VMEM] + [ANY] * len(after),
        out_specs=VMEM,
        compiler_params=params(8),
        cost_estimate=cost(0, 6 * near.size),
    )(place, near, far, *after)


def embed_kernel(count, chips, block, first, exclusive, place_ref, onehot_ref, table_ref, *refs):
    rows_ref = refs[-1]
    size = rows_ref.shape[0] // count
    x, core = place_ref[0] // 2, lax.rem(place_ref[0], 2)
    for held in range(count):
        dest = lax.bitwise_xor(place_ref[1], held) if exclusive else held
        ahead = lax.rem(dest // 2 - x + 2 * chips - 1, chips)
        slot = jnp.where(core == lax.rem(dest, 2), chips, 0) + ahead
        here = pl.ds(pl.multiple_of(dest * block + first, 16), size)
        looked = jnp.dot(onehot_ref[here, :], table_ref[...], preferred_element_type=F32)
        total = refs[held][...].astype(F32) + looked
        rows_ref[pl.ds(pl.multiple_of(slot * size, 16), size), :] = total.astype(BF16)


def embed(chips, block, first, exclusive, place, onehot, table, held, after):
    count = len(held)
    size, depth = held[0].shape
    tile = divisor(depth, (896, 512, 256, 128))
    piece = pl.BlockSpec((size, tile), lambda j: (0, j))
    return pl.pallas_call(
        functools.partial(embed_kernel, count, chips, block, first, exclusive),
        name="embed",
        grid=(depth // tile,),
        out_shape=jax.ShapeDtypeStruct((count * size, depth), BF16),
        in_specs=[SMEM, pl.BlockSpec(onehot.shape, lambda j: (0, 0)), pl.BlockSpec((table.shape[0], tile), lambda j: (0, j))]
        + [piece] * count + [ANY] * len(after),
        out_specs=pl.BlockSpec((count * size, tile), lambda j: (0, j)),
        compiler_params=params(16),
        cost_estimate=cost(2 * count * size * table.shape[0] * depth, 6 * count * size * depth),
    )(place, onehot, table, *held, *after)


def product_kernel(start, tile, steps, slots, rows_ref, weight_ref, *refs):
    send_ref, keep_ref, held, arrived = refs[-4:]
    half = send_ref.shape[0]
    step = pl.program_id(0)

    def fetch(index):
        column = pl.multiple_of(start + index * tile, 128)
        slot = lax.rem(index, slots)
        return pltpu.make_async_copy(weight_ref.at[:, pl.ds(column, tile)], held.at[slot], arrived.at[slot])

    @pl.when(step == 0)
    def _():
        for index in range(min(slots - 1, steps)):
            fetch(index).start()

    @pl.when(step + slots - 1 < steps)
    def _():
        fetch(step + slots - 1).start()

    fetch(step).wait()
    out = jnp.dot(rows_ref[...], held[lax.rem(step, slots)], preferred_element_type=F32)
    send_ref[...] = out[:half].astype(BF16)
    keep_ref[...] = out[half:].astype(BF16)


def product(rows, weight, start, width, after):
    height, depth = rows.shape
    tile = divisor(width, (512, 384, 256, 128))
    slots = 4
    half = jax.ShapeDtypeStruct((height // 2, width), BF16)
    return pl.pallas_call(
        functools.partial(product_kernel, start, tile, width // tile, slots),
        name="product",
        grid=(width // tile,),
        out_shape=[half, half],
        in_specs=[pl.BlockSpec((height, depth), lambda j: (0, 0))] + [ANY] * (1 + len(after)),
        out_specs=[pl.BlockSpec((height // 2, tile), lambda j: (0, j))] * 2,
        scratch_shapes=[pltpu.VMEM((slots, depth, tile), BF16), pltpu.SemaphoreType.DMA((slots,))],
        compiler_params=params(32),
        cost_estimate=cost(2 * height * depth * width, 2 * (height * depth + depth * width + height * width)),
    )(rows, weight, *after)


def pair_kernel(keep_ref, got_ref, *refs):
    away_ref, stay_ref = refs[-2:]
    cut = away_ref.shape[0]
    total = keep_ref[...].astype(F32) + got_ref[...].astype(F32)
    away_ref[...] = total[:cut].astype(BF16)
    stay_ref[...] = total[cut:].astype(BF16)


def pair(chips, keep, got, after):
    height, width = keep.shape
    size = height // chips
    tile = divisor(width, (1536, 1152, 768, 512, 384, 256, 128))
    spec = lambda rows: pl.BlockSpec((rows, tile), lambda j: (0, j))
    return pl.pallas_call(
        pair_kernel,
        name="pair",
        grid=(width // tile,),
        out_shape=[jax.ShapeDtypeStruct((height - size, width), BF16), jax.ShapeDtypeStruct((size, width), BF16)],
        in_specs=[spec(height), spec(height)] + [ANY] * len(after),
        out_specs=[spec(height - size), spec(size)],
        compiler_params=params(16),
        cost_estimate=cost(height * width, 6 * height * width),
    )(keep, got, *after)


def finish_kernel(count, *refs):
    total = refs[0][...].astype(F32)
    for index in range(1, count):
        total = total + refs[index][...].astype(F32)
    out_ref, token_ref = refs[-2:]
    out_ref[...] = jax.nn.gelu(total, approximate=True).astype(BF16)
    token_ref[...] = jnp.zeros_like(token_ref)


def finish(shape, step, rows, terms, held, after):
    index, start, width = step
    tile = divisor(width, (1536, 1152, 768, 512, 384, 256, 128))
    aliases = {} if held is None else {len(terms): 0}
    return pl.pallas_call(
        functools.partial(finish_kernel, len(terms)),
        name="finish",
        grid=(width // tile,),
        out_shape=[jax.ShapeDtypeStruct(shape, BF16), jax.ShapeDtypeStruct((8, 128), F32)],
        in_specs=[pl.BlockSpec((rows, tile), lambda j: (0, j))] * len(terms) + [ANY] * (len(aliases) + len(after)),
        out_specs=[
            pl.BlockSpec((rows, tile), lambda j: (index, start // tile + j)),
            pl.BlockSpec((8, 128), lambda j: (0, 0)),
        ],
        input_output_aliases=aliases,
        compiler_params=params(16),
        cost_estimate=cost(12 * rows * width, 6 * rows * width),
    )(*terms, *([] if held is None else [held]), *after)


EARLY = (1, 1)
LAG = 3
LAST = (1, 1, 2, 2)


def column_pieces(columns, shares):
    unit, start, pieces = columns // sum(shares), 0, []
    for share in shares:
        pieces.append((start, share * unit))
        start += share * unit
    return pieces


def local(n_gx, n_gy, hidden, parents, depth_table, weight):
    tree = depth_table.shape[0]
    columns = weight.shape[1]
    block = hidden.shape[0]
    chips = n_gx // 2
    place = jnp.stack([lax.axis_index("gx"), lax.axis_index("gy")]).astype(jnp.int32)
    onehot = depth_onehot(parents, tree)

    parts = divisor(block // 16, (3, 4, 2))
    size = block // parts
    own = [hidden[index * size:(index + 1) * size] for index in range(parts)]

    exclusive = n_gy == 4
    if exclusive:
        near = [None] * parts
        far = [None] * parts
        rest = [None] * parts

        def swap(array, distance):
            return lax.ppermute(array, "gy", [(k, k ^ distance) for k in range(n_gy)])

        near[0], far[0] = swap(own[0], 1), swap(own[0], 2)
        if parts > 1:
            near[1] = swap(own[1], 1)
    else:
        gathered = [lax.all_gather(rows, "gy", axis=0) for rows in own]

    def pass_on(index, after):
        if not exclusive or index >= parts:
            return []
        given = forward(place, near[index], far[index], after)
        rest[index] = lax.ppermute(given, "gy", [(0, 2), (1, 0), (2, 3), (3, 1)])
        if index == 0 and parts > 1:
            far[1] = swap(lax.optimization_barrier((own[1], given))[0], 2)
        return [given]

    sibling = [(g, g ^ 1) for g in range(n_gx)]

    def across(ahead):
        return [(g, (g // 2 + ahead) % chips * 2 + g % 2) for g in range(n_gx)]

    def exchange(away, stay):
        return [stay] + [
            lax.ppermute(away[(ahead - 1) * size:ahead * size], "gx", across(ahead)) for ahead in range(1, chips)
        ]

    steps = [
        (index, start, width)
        for index in range(parts)
        for start, width in column_pieces(columns, LAST if index == parts - 1 else EARLY)
    ]
    out = None
    products, sums = [], []
    pass_on(0, [])
    for step, (index, start, width) in enumerate(steps):
        after = [products[-1][0]] if products else []
        before = []
        if start == 0:
            if exclusive:
                held = [own[index], near[index], far[index], rest[index]]
            else:
                held = [gathered[index][k] for k in range(n_gy)]
            rows = embed(chips, block, index * size, exclusive, place, onehot, depth_table, held, after)
        elif start == steps[step - 1][2] and index + 1 < parts:
            before += pass_on(index + 1, after)
        if step >= 2:
            away, stay = pair(chips, *products[step - 2], after)
            before.append(stay)
            sums.append(exchange(away, stay))
        if step >= LAG:
            out, token = finish((block, columns), steps[step - LAG], size, sums[step - LAG], out, after)
            before.append(token)
        send, keep = product(rows, weight, start, width, before)
        products.append((keep, lax.ppermute(send, "gx", sibling)))
        if exclusive and start > 0 and index + 2 < parts and near[index + 2] is None:
            rows_on, _ = lax.optimization_barrier((own[index + 2], keep))
            near[index + 2], far[index + 2] = swap(rows_on, 1), swap(rows_on, 2)
    token = []
    for step in range(len(steps) - LAG, len(steps)):
        for ready in range(len(sums), min(step + 2, len(steps))):
            sums.append(exchange(*pair(chips, *products[ready], token)))
        out, done = finish((block, columns), steps[step], size, sums[step], out, [])
        token = [done]
    return out


def solution(mesh):
    return jax.shard_map(
        functools.partial(local, mesh.shape["gx"], mesh.shape["gy"]),
        mesh=mesh,
        in_specs=(P(("grp", "gy"), "gx"), P("grp"), P(None, "gx"), P("gx", "gy")),
        out_specs=P(("grp", "gx"), "gy"),
        check_vma=False,
    )
```

```python
import functools

import jax
import jax.numpy as jnp
from jax import lax
from jax.experimental import pallas as pl
from jax.experimental.pallas import tpu as pltpu
from jax.sharding import PartitionSpec as P

BF16 = jnp.bfloat16
F32 = jnp.float32
MIB = 1024 * 1024
ANY = pl.BlockSpec(memory_space=pl.ANY)
VMEM = pl.BlockSpec(memory_space=pltpu.VMEM)
SMEM = pl.BlockSpec(memory_space=pltpu.SMEM)


def params(limit):
    return pltpu.CompilerParams(vmem_limit_bytes=limit * MIB)


def cost(flops, accessed):
    return pl.CostEstimate(flops=8 * flops, bytes_accessed=8 * accessed, transcendentals=0)


def divisor(extent, choices):
    for choice in choices:
        if extent % choice == 0:
            return choice
    return extent


def onehot_kernel(tree, parents_ref, onehot_ref):
    lanes = lax.broadcasted_iota(jnp.int32, (tree, tree), 1)
    rows = lax.broadcasted_iota(jnp.int32, (tree, 1), 0)
    firsts = range(0, onehot_ref.shape[0], tree)
    parents = [parents_ref[first:first + tree, :] - first for first in firsts]
    jumps = [(parent == lanes).astype(BF16) for parent in parents]
    depths = [jnp.broadcast_to((parent != rows).astype(F32), (tree, 128)) for parent in parents]
    for level in range((tree - 1).bit_length()):
        depths = [
            depth + jnp.dot(jump, depth.astype(BF16), preferred_element_type=F32)
            for depth, jump in zip(depths, jumps)
        ]
        jumps = [jnp.dot(jump, jump, preferred_element_type=F32).astype(BF16) for jump in jumps]
    for first, depth in zip(firsts, depths):
        onehot_ref[first:first + tree, :] = (depth[:, :1].astype(jnp.int32) == lanes).astype(BF16)


def depth_onehot(parents, tree):
    rows = parents.shape[0]
    return pl.pallas_call(
        functools.partial(onehot_kernel, tree),
        name="onehot",
        out_shape=jax.ShapeDtypeStruct((rows, tree), BF16),
        compiler_params=params(16),
        cost_estimate=cost(48 * rows * tree * tree, 8 * rows * tree),
    )(parents[:, None])


def forward_kernel(place_ref, near_ref, far_ref, *refs):
    out_ref = refs[-1]
    outer = jnp.logical_or(place_ref[1] == 0, place_ref[1] == 3)

    @pl.when(outer)
    def _():
        out_ref[...] = near_ref[...]

    @pl.when(jnp.logical_not(outer))
    def _():
        out_ref[...] = far_ref[...]


def forward(place, near, far, after):
    return pl.pallas_call(
        forward_kernel,
        name="forward",
        out_shape=jax.ShapeDtypeStruct(near.shape, near.dtype),
        in_specs=[SMEM, VMEM, VMEM] + [ANY] * len(after),
        out_specs=VMEM,
        compiler_params=params(8),
        cost_estimate=cost(0, 6 * near.size),
    )(place, near, far, *after)


def slot_of(dest, chips, gx):
    ahead = lax.rem(dest // 2 - gx // 2 + 2 * chips - 1, chips)
    return jnp.where(lax.rem(gx, 2) == lax.rem(dest, 2), chips, 0) + ahead


def embed_kernel(count, chips, block, first, exclusive, place_ref, onehot_ref, table_ref, *refs):
    rows_ref = refs[-1]
    size = rows_ref.shape[0] // count
    for held in range(count):
        dest = lax.bitwise_xor(place_ref[1], held) if exclusive else held
        slot = slot_of(dest, chips, place_ref[0])
        here = pl.ds(pl.multiple_of(dest * block + first, 16), size)
        looked = jnp.dot(onehot_ref[here, :], table_ref[...], preferred_element_type=F32)
        total = refs[held][...].astype(F32) + looked
        rows_ref[pl.ds(pl.multiple_of(slot * size, 16), size), :] = total.astype(BF16)


def embed(chips, block, first, exclusive, place, onehot, table, held, after):
    count = len(held)
    size, depth = held[0].shape
    tile = divisor(depth, (896, 512, 256, 128))
    piece = pl.BlockSpec((size, tile), lambda j: (0, j))
    return pl.pallas_call(
        functools.partial(embed_kernel, count, chips, block, first, exclusive),
        name="embed",
        grid=(depth // tile,),
        out_shape=jax.ShapeDtypeStruct((count * size, depth), BF16),
        in_specs=[SMEM, pl.BlockSpec(onehot.shape, lambda j: (0, 0)), pl.BlockSpec((table.shape[0], tile), lambda j: (0, j))]
        + [piece] * count + [ANY] * len(after),
        out_specs=pl.BlockSpec((count * size, tile), lambda j: (0, j)),
        compiler_params=params(16),
        cost_estimate=cost(2 * count * size * table.shape[0] * depth, 6 * count * size * depth),
    )(place, onehot, table, *held, *after)


def embed_own_kernel(block, first, place_ref, onehot_ref, table_ref, hidden_ref, *refs):
    start = place_ref[1] * block
    for rows_ref in refs:
        size = rows_ref.shape[0]
        here = pl.ds(pl.multiple_of(start + first, 16), size)
        looked = jnp.dot(onehot_ref[here, :], table_ref[...], preferred_element_type=F32)
        rows_ref[...] = (hidden_ref[first:first + size, :].astype(F32) + looked).astype(BF16)
        first += size


def embed_own(first, size, count, place, onehot, table, hidden):
    block, depth = hidden.shape
    tile = divisor(depth, (896, 512, 256, 128))
    column = lambda j: (0, j)
    return pl.pallas_call(
        functools.partial(embed_own_kernel, block, first),
        name="own",
        grid=(depth // tile,),
        out_shape=[jax.ShapeDtypeStruct((size, depth), BF16)] * count,
        in_specs=[
            SMEM,
            pl.BlockSpec(onehot.shape, lambda j: (0, 0)),
            pl.BlockSpec((table.shape[0], tile), column),
            pl.BlockSpec((block, tile), column),
        ],
        out_specs=[pl.BlockSpec((size, tile), column)] * count,
        compiler_params=params(16),
        cost_estimate=cost(2 * count * size * table.shape[0] * depth, 6 * count * size * depth),
    )(place, onehot, table, hidden)


def gelu_sum(terms):
    total = terms[0].astype(F32)
    for term in terms[1:]:
        total = total + term.astype(F32)
    return jax.nn.gelu(total, approximate=True).astype(BF16)


def product_kernel(start, tile, steps, slots, chips, count, exclusive, ending, place_ref, weight_ref, *refs):
    blocks = refs[:count]
    terms = refs[count:count + ending[3]]
    outs = 2 if not ending[3] else 3
    scratch = len(refs) - (4 if not ending[3] else 8)
    send_ref, keep_ref = refs[scratch - outs:scratch - outs + 2]
    rows, held, arrived, filled = refs[scratch:scratch + 4]
    half = send_ref.shape[0]
    step = pl.program_id(0)

    def fetch(index):
        column = pl.multiple_of(start + index * tile, 128)
        slot = lax.rem(index, slots)
        return pltpu.make_async_copy(weight_ref.at[:, pl.ds(column, tile)], held.at[slot], arrived.at[slot])

    def fill(index):
        if count == 1:
            return pltpu.make_async_copy(blocks[0], rows, filled.at[0])
        size = rows.shape[0] // count
        dest = lax.bitwise_xor(place_ref[1], index) if exclusive else index
        first = pl.multiple_of(slot_of(dest, chips, place_ref[0]) * size, 16)
        return pltpu.make_async_copy(blocks[index], rows.at[pl.ds(first, size), :], filled.at[index])

    if ending[3]:
        out_ref = refs[scratch - 1]
        term_buffer, out_buffer, term_sems, out_sem = refs[scratch + 4:]
        row, column, width, number = ending
        given = [pltpu.make_async_copy(terms[n], term_buffer.at[n], term_sems.at[n]) for n in range(number)]
        place_out = out_ref.at[row:row + out_buffer.shape[0], column:column + width]
        taken = pltpu.make_async_copy(out_buffer, place_out, out_sem.at[0])

    @pl.when(step == 0)
    def _():
        fetch(0).start()
        for index in range(count):
            fill(index).start()
        for index in range(1, min(slots - 1, steps)):
            fetch(index).start()
        if ending[3]:
            for copy in given:
                copy.start()
        for index in range(count):
            fill(index).wait()

    @pl.when(step + slots - 1 < steps)
    def _():
        fetch(step + slots - 1).start()

    fetch(step).wait()
    out = jnp.dot(rows[...], held[lax.rem(step, slots)], preferred_element_type=F32)
    send_ref[...] = out[:half].astype(BF16)
    keep_ref[...] = out[half:].astype(BF16)

    if ending[3]:
        @pl.when(step == 0)
        def _():
            for copy in given:
                copy.wait()
            part = divisor(width, (512, 384, 256, 128))

            @pl.loop(0, width // part)
            def _(index):
                here = pl.ds(pl.multiple_of(index * part, 128), part)
                out_buffer[:, here] = gelu_sum([term_buffer[n, :, here] for n in range(number)])

            taken.start()

        @pl.when(step == steps - 1)
        def _():
            taken.wait()


def product(chips, exclusive, place, blocks, weight, start, width, after, ending=None, terms=(), out=None, shape=None):
    count = len(blocks)
    height, depth = count * blocks[0].shape[0], blocks[0].shape[1]
    tile = divisor(width, (512, 384, 256, 128))
    slots = 4
    half = jax.ShapeDtypeStruct((height // 2, width), BF16)
    outs = [half, half]
    out_specs = [pl.BlockSpec((height // 2, tile), lambda j: (0, j))] * 2
    scratch = [
        pltpu.VMEM((height, depth), BF16),
        pltpu.VMEM((slots, depth, tile), BF16),
        pltpu.SemaphoreType.DMA((slots,)),
        pltpu.SemaphoreType.DMA((count,)),
    ]
    operands = [place, weight, *blocks, *terms]
    aliases = {}
    ending = (0, 0, 0, 0) if not terms else (*ending, terms[0].shape[1], len(terms))
    if terms:
        outs.append(jax.ShapeDtypeStruct(shape, BF16))
        out_specs.append(ANY)
        scratch += [
            pltpu.VMEM((len(terms), *terms[0].shape), BF16),
            pltpu.VMEM(terms[0].shape, BF16),
            pltpu.SemaphoreType.DMA((len(terms),)),
            pltpu.SemaphoreType.DMA((1,)),
        ]
        if out is not None:
            aliases = {len(operands): 2}
            operands.append(out)
    operands += after
    return pl.pallas_call(
        functools.partial(product_kernel, start, tile, width // tile, slots, chips, count, exclusive, ending),
        name="product",
        grid=(width // tile,),
        out_shape=outs,
        in_specs=[SMEM] + [ANY] * (len(operands) - 1),
        out_specs=out_specs,
        scratch_shapes=scratch,
        input_output_aliases=aliases,
        compiler_params=params(40),
        cost_estimate=cost(2 * height * depth * width, 2 * (height * depth + depth * width + height * width)),
    )(*operands)


def pair_kernel(keep_ref, got_ref, *refs):
    away_ref, stay_ref = refs[-2:]
    cut = away_ref.shape[0]
    total = keep_ref[...].astype(F32) + got_ref[...].astype(F32)
    away_ref[...] = total[:cut].astype(BF16)
    stay_ref[...] = total[cut:].astype(BF16)


def pair(chips, keep, got, after):
    height, width = keep.shape
    size = height // chips
    tile = divisor(width, (1536, 1152, 768, 512, 384, 256, 128))
    spec = lambda rows: pl.BlockSpec((rows, tile), lambda j: (0, j))
    return pl.pallas_call(
        pair_kernel,
        name="pair",
        grid=(width // tile,),
        out_shape=[jax.ShapeDtypeStruct((height - size, width), BF16), jax.ShapeDtypeStruct((size, width), BF16)],
        in_specs=[spec(height), spec(height)] + [ANY] * len(after),
        out_specs=[spec(height - size), spec(size)],
        compiler_params=params(16),
        cost_estimate=cost(height * width, 6 * height * width),
    )(keep, got, *after)


def finish_kernel(count, *refs):
    out_ref, token_ref = refs[-2:]
    out_ref[...] = gelu_sum([refs[index][...] for index in range(count)])
    token_ref[...] = jnp.zeros_like(token_ref)


def finish(shape, step, rows, terms, held, after):
    index, start, width = step
    tile = divisor(width, (1536, 1152, 768, 512, 384, 256, 128))
    aliases = {} if held is None else {len(terms): 0}
    return pl.pallas_call(
        functools.partial(finish_kernel, len(terms)),
        name="finish",
        grid=(width // tile,),
        out_shape=[jax.ShapeDtypeStruct(shape, BF16), jax.ShapeDtypeStruct((8, 128), F32)],
        in_specs=[pl.BlockSpec((rows, tile), lambda j: (0, j))] * len(terms) + [ANY] * (len(aliases) + len(after)),
        out_specs=[
            pl.BlockSpec((rows, tile), lambda j: (index, start // tile + j)),
            pl.BlockSpec((8, 128), lambda j: (0, 0)),
        ],
        input_output_aliases=aliases,
        compiler_params=params(16),
        cost_estimate=cost(12 * rows * width, 6 * rows * width),
    )(*terms, *([] if held is None else [held]), *after)


def column_pieces(columns, shares):
    unit, start, pieces = columns // sum(shares), 0, []
    for share in shares:
        pieces.append((start, share * unit))
        start += share * unit
    return pieces


SHARES = ((3, 3), (3, 3), (2, 2, 2))

ORDER = "f0 p00 f1 p01 t2 s00 p10 s01 f2 p11-00 s10 p20-01 s11 p21-10 s20 p22-11 s21 g20 s22 g21 g22".split()


def local(n_gx, n_gy, hidden, parents, depth_table, weight):
    tree = depth_table.shape[0]
    columns = weight.shape[1]
    block = hidden.shape[0]
    chips = n_gx // 2
    parts = len(SHARES)
    size = block // parts
    place = jnp.stack([lax.axis_index("gx"), lax.axis_index("gy")]).astype(jnp.int32)

    exclusive = n_gy == 4

    def swap(array, distance):
        return lax.ppermute(array, "gy", [(k, k ^ distance) for k in range(n_gy)])

    def later(array, token):
        return lax.optimization_barrier((array, token))[0]

    def take(index, token):
        if not exclusive:
            whole = lax.all_gather(own[index], "gy", axis=0)
            held[index] = [whole[k] for k in range(n_gy)]
        else:
            rows = own[index] if token is None else later(own[index], token)
            held[index] = [own[index], swap(rows, 1), swap(rows, 2)]

    own, held = [hidden[:size]], [None] * parts
    take(0, None)
    onehot = depth_onehot(parents, tree)
    own += embed_own(size, size, parts - 1, place, onehot, depth_table, hidden)

    sibling = [(g, g ^ 1) for g in range(n_gx)]

    def across(ahead):
        return [(g, (g // 2 + ahead) % chips * 2 + g % 2) for g in range(n_gx)]

    out, after = None, own[1:2]
    pieces = [column_pieces(columns, shares) for shares in SHARES]
    products, sums = {}, {}
    for item in ORDER:
        kind, index, piece = item[0], int(item[1]), item[1:3]
        if kind == "f":
            if exclusive:
                given = forward(place, held[index][1], held[index][2], after)
                held[index].append(lax.ppermute(given, "gy", [(0, 2), (1, 0), (2, 3), (3, 1)]))
                after = [given]
            if index == 0:
                take(1, after[0] if after else None)
                rows = embed(chips, block, 0, exclusive, place, onehot, depth_table, held[0], after)
                held[0] = [rows]
        if kind == "t":
            take(index, after[0])
        if kind == "p":
            start, width = pieces[index][int(item[2])]
            extra = {}
            if len(item) > 3:
                done = item[4:]
                ending = (int(done[0]) * size, pieces[int(done[0])][int(done[1])][0])
                extra = dict(ending=ending, terms=sums[done], out=out, shape=(block, columns))
            send, keep, *rest = product(chips, exclusive, place, held[index], weight, start, width, after, **extra)
            out = rest[0] if rest else out
            products[piece] = (keep, lax.ppermute(send, "gx", sibling))
            after = [keep]
        if kind == "s":
            away, stay = pair(chips, *products[piece], after)
            sums[piece] = [stay] + [
                lax.ppermute(away[(ahead - 1) * size:ahead * size], "gx", across(ahead)) for ahead in range(1, chips)
            ]
            after = [stay]
        if kind == "g":
            start, width = pieces[index][int(item[2])]
            out, token = finish((block, columns), (index, start, width), size, sums[piece], out, after)
            after = [token]
    return out


def solution(mesh):
    return jax.shard_map(
        functools.partial(local, mesh.shape["gx"], mesh.shape["gy"]),
        mesh=mesh,
        in_specs=(P(("grp", "gy"), "gx"), P("grp"), P(None, "gx"), P("gx", "gy")),
        out_specs=P(("grp", "gx"), "gy"),
        check_vma=False,
    )
```

```python
import functools

import jax
import jax.numpy as jnp
from jax import lax
from jax.experimental import pallas as pl
from jax.experimental.pallas import tpu as pltpu
from jax.sharding import PartitionSpec as P

BF16 = jnp.bfloat16
F32 = jnp.float32
MIB = 1024 * 1024
ANY = pl.BlockSpec(memory_space=pl.ANY)
VMEM = pl.BlockSpec(memory_space=pltpu.VMEM)
SMEM = pl.BlockSpec(memory_space=pltpu.SMEM)


def params(limit):
    return pltpu.CompilerParams(vmem_limit_bytes=limit * MIB)


def cost(flops, accessed, long=False):
    factor = 1000 if long else 8
    return pl.CostEstimate(flops=factor * flops, bytes_accessed=factor * accessed, transcendentals=0)


def divisor(extent, choices):
    for choice in choices:
        if extent % choice == 0:
            return choice
    return extent


def onehot_kernel(tree, parents_ref, onehot_ref):
    lanes = lax.broadcasted_iota(jnp.int32, (tree, tree), 1)
    rows = lax.broadcasted_iota(jnp.int32, (tree, 1), 0)
    firsts = range(0, onehot_ref.shape[0], tree)
    parents = [parents_ref[first:first + tree, :] - first for first in firsts]
    jumps = [(parent == lanes).astype(BF16) for parent in parents]
    depths = [jnp.broadcast_to((parent != rows).astype(F32), (tree, 128)) for parent in parents]
    for level in range((tree - 1).bit_length()):
        depths = [
            depth + jnp.dot(jump, depth.astype(BF16), preferred_element_type=F32)
            for depth, jump in zip(depths, jumps)
        ]
        jumps = [jnp.dot(jump, jump, preferred_element_type=F32).astype(BF16) for jump in jumps]
    for first, depth in zip(firsts, depths):
        onehot_ref[first:first + tree, :] = (depth[:, :1].astype(jnp.int32) == lanes).astype(BF16)


def depth_onehot(parents, tree):
    rows = parents.shape[0]
    return pl.pallas_call(
        functools.partial(onehot_kernel, tree),
        name="onehot",
        out_shape=jax.ShapeDtypeStruct((rows, tree), BF16),
        compiler_params=params(16),
        cost_estimate=cost(48 * rows * tree * tree, 8 * rows * tree),
    )(parents[:, None])


def forward_kernel(place_ref, near_ref, far_ref, *refs):
    out_ref = refs[-1]
    outer = jnp.logical_or(place_ref[1] == 0, place_ref[1] == 3)

    @pl.when(outer)
    def _():
        out_ref[...] = near_ref[...]

    @pl.when(jnp.logical_not(outer))
    def _():
        out_ref[...] = far_ref[...]


def forward(place, near, far, after, long):
    return pl.pallas_call(
        forward_kernel,
        name="forward",
        out_shape=jax.ShapeDtypeStruct(near.shape, near.dtype),
        in_specs=[SMEM, VMEM, VMEM] + [ANY] * len(after),
        out_specs=VMEM,
        compiler_params=params(8),
        cost_estimate=cost(0, 6 * near.size, long),
    )(place, near, far, *after)


def slot_of(dest, chips, gx):
    ahead = lax.rem(dest // 2 - gx // 2 + 2 * chips - 1, chips)
    return jnp.where(lax.rem(gx, 2) == lax.rem(dest, 2), chips, 0) + ahead


def embed_kernel(count, chips, block, first, exclusive, place_ref, onehot_ref, table_ref, *refs):
    rows_ref = refs[-1]
    size = rows_ref.shape[0] // count
    for held in range(count):
        dest = lax.bitwise_xor(place_ref[1], held) if exclusive else held
        slot = slot_of(dest, chips, place_ref[0])
        here = pl.ds(pl.multiple_of(dest * block + first, 16), size)
        looked = jnp.dot(onehot_ref[here, :], table_ref[...], preferred_element_type=F32)
        total = refs[held][...].astype(F32) + looked
        rows_ref[pl.ds(pl.multiple_of(slot * size, 16), size), :] = total.astype(BF16)


def embed(chips, block, first, exclusive, place, onehot, table, held, after):
    count = len(held)
    size, depth = held[0].shape
    tile = divisor(depth, (896, 512, 256, 128))
    piece = pl.BlockSpec((size, tile), lambda j: (0, j))
    return pl.pallas_call(
        functools.partial(embed_kernel, count, chips, block, first, exclusive),
        name="embed",
        grid=(depth // tile,),
        out_shape=jax.ShapeDtypeStruct((count * size, depth), BF16),
        in_specs=[SMEM, pl.BlockSpec(onehot.shape, lambda j: (0, 0)), pl.BlockSpec((table.shape[0], tile), lambda j: (0, j))]
        + [piece] * count + [ANY] * len(after),
        out_specs=pl.BlockSpec((count * size, tile), lambda j: (0, j)),
        compiler_params=params(16),
        cost_estimate=cost(2 * count * size * table.shape[0] * depth, 6 * count * size * depth),
    )(place, onehot, table, *held, *after)


def embed_own_kernel(block, first, place_ref, onehot_ref, table_ref, hidden_ref, *refs):
    start = place_ref[1] * block
    for rows_ref in refs:
        size = rows_ref.shape[0]
        here = pl.ds(pl.multiple_of(start + first, 16), size)
        looked = jnp.dot(onehot_ref[here, :], table_ref[...], preferred_element_type=F32)
        rows_ref[...] = (hidden_ref[first:first + size, :].astype(F32) + looked).astype(BF16)
        first += size


def embed_own(first, size, count, place, onehot, table, hidden):
    block, depth = hidden.shape
    tile = divisor(depth, (896, 512, 256, 128))
    column = lambda j: (0, j)
    return pl.pallas_call(
        functools.partial(embed_own_kernel, block, first),
        name="own",
        grid=(depth // tile,),
        out_shape=[jax.ShapeDtypeStruct((size, depth), BF16)] * count,
        in_specs=[
            SMEM,
            pl.BlockSpec(onehot.shape, lambda j: (0, 0)),
            pl.BlockSpec((table.shape[0], tile), column),
            pl.BlockSpec((block, tile), column),
        ],
        out_specs=[pl.BlockSpec((size, tile), column)] * count,
        compiler_params=params(16),
        cost_estimate=cost(2 * count * size * table.shape[0] * depth, 6 * count * size * depth),
    )(place, onehot, table, hidden)


def gelu_sum(terms):
    total = terms[0].astype(F32)
    for term in terms[1:]:
        total = total + term.astype(F32)
    return jax.nn.gelu(total, approximate=True).astype(BF16)


def product_kernel(start, tile, steps, slots, chips, count, exclusive, ending, place_ref, weight_ref, *refs):
    blocks = refs[:count]
    terms = refs[count:count + ending[3]]
    outs = 2 if not ending[3] else 3
    scratch = len(refs) - (3 if not ending[3] else 7)
    send_ref, keep_ref = refs[scratch - outs:scratch - outs + 2]
    rows, held, arrived = refs[scratch:scratch + 3]
    half = send_ref.shape[0]
    step = pl.program_id(0)
    lanes = held.shape[3]

    def fetch(index):
        slot = lax.rem(index, slots)
        for side in range(tile // lanes):
            column = pl.multiple_of(start + index * tile + side * lanes, 128)
            yield pltpu.make_async_copy(weight_ref.at[:, pl.ds(column, lanes)], held.at[slot, side], arrived.at[slot, side])

    if ending[3]:
        out_ref = refs[scratch - 1]
        term_buffer, out_buffer, term_sems, out_sem = refs[scratch + 3:]
        row, column, width, number = ending
        given = [pltpu.make_async_copy(terms[n], term_buffer.at[n], term_sems.at[n]) for n in range(number)]
        place_out = out_ref.at[row:row + out_buffer.shape[0], column:column + width]
        taken = pltpu.make_async_copy(out_buffer, place_out, out_sem.at[0])

    @pl.when(step == 0)
    def _():
        for index in range(min(slots - 1, steps)):
            for copy in fetch(index):
                copy.start()
        if ending[3]:
            for copy in given:
                copy.start()
        size = rows.shape[0] // count
        for index in range(count):
            first = 0
            if count > 1:
                dest = lax.bitwise_xor(place_ref[1], index) if exclusive else index
                first = pl.multiple_of(slot_of(dest, chips, place_ref[0]) * size, 16)
            rows[pl.ds(first, size), :] = blocks[index][...]

    @pl.when(step + slots - 1 < steps)
    def _():
        for copy in fetch(step + slots - 1):
            copy.start()

    for side, copy in enumerate(fetch(step)):
        copy.wait()
        out = jnp.dot(rows[...], held[lax.rem(step, slots), side], preferred_element_type=F32)
        here = slice(side * lanes, (side + 1) * lanes)
        send_ref[:, here] = out[:half].astype(BF16)
        keep_ref[:, here] = out[half:].astype(BF16)

    if ending[3]:
        @pl.when(step == 0)
        def _():
            for copy in given:
                copy.wait()
            part = divisor(width, (512, 384, 256, 128))

            @pl.loop(0, width // part)
            def _(index):
                here = pl.ds(pl.multiple_of(index * part, 128), part)
                out_buffer[:, here] = gelu_sum([term_buffer[n, :, here] for n in range(number)])

            taken.start()

        @pl.when(step == steps - 1)
        def _():
            taken.wait()


def product(chips, exclusive, place, blocks, weight, start, width, after, ending=None, terms=(), out=None, shape=None):
    count = len(blocks)
    height, depth = count * blocks[0].shape[0], blocks[0].shape[1]
    tile = divisor(width, (512, 384, 256, 128))
    lanes = divisor(tile, (256, 128))
    slots = 4
    half = jax.ShapeDtypeStruct((height // 2, width), BF16)
    outs = [half, half]
    out_specs = [pl.BlockSpec((height // 2, tile), lambda j: (0, j))] * 2
    scratch = [
        pltpu.VMEM((height, depth), BF16),
        pltpu.VMEM((slots, tile // lanes, depth, lanes), BF16),
        pltpu.SemaphoreType.DMA((slots, tile // lanes)),
    ]
    operands = [place, weight, *blocks, *terms]
    aliases = {}
    ending = (0, 0, 0, 0) if not terms else (*ending, terms[0].shape[1], len(terms))
    if terms:
        outs.append(jax.ShapeDtypeStruct(shape, BF16))
        out_specs.append(ANY)
        scratch += [
            pltpu.VMEM((len(terms), *terms[0].shape), BF16),
            pltpu.VMEM(terms[0].shape, BF16),
            pltpu.SemaphoreType.DMA((len(terms),)),
            pltpu.SemaphoreType.DMA((1,)),
        ]
        if out is not None:
            aliases = {len(operands): 2}
            operands.append(out)
    operands += after
    return pl.pallas_call(
        functools.partial(product_kernel, start, tile, width // tile, slots, chips, count, exclusive, ending),
        name="product",
        grid=(width // tile,),
        out_shape=outs,
        in_specs=[SMEM, ANY] + [VMEM] * count + [ANY] * (len(operands) - 2 - count),
        out_specs=out_specs,
        scratch_shapes=scratch,
        input_output_aliases=aliases,
        compiler_params=params(40),
        cost_estimate=cost(2 * height * depth * width, 2 * (height * depth + depth * width + height * width)),
    )(*operands)


def pair_kernel(keep_ref, got_ref, *refs):
    away_ref, stay_ref = refs[-2:]
    cut = away_ref.shape[0]
    total = keep_ref[...].astype(F32) + got_ref[...].astype(F32)
    away_ref[...] = total[:cut].astype(BF16)
    stay_ref[...] = total[cut:].astype(BF16)


def pair(chips, keep, got, after, long):
    height, width = keep.shape
    size = height // chips
    tile = divisor(width, (1536, 1152, 768, 512, 384, 256, 128))
    spec = lambda rows: pl.BlockSpec((rows, tile), lambda j: (0, j))
    return pl.pallas_call(
        pair_kernel,
        name="pair",
        grid=(width // tile,),
        out_shape=[jax.ShapeDtypeStruct((height - size, width), BF16), jax.ShapeDtypeStruct((size, width), BF16)],
        in_specs=[spec(height), spec(height)] + [ANY] * len(after),
        out_specs=[spec(height - size), spec(size)],
        compiler_params=params(16),
        cost_estimate=cost(height * width, 6 * height * width, long),
    )(keep, got, *after)


def finish_kernel(count, *refs):
    out_ref, token_ref = refs[-2:]
    out_ref[...] = gelu_sum([refs[index][...] for index in range(count)])
    token_ref[...] = jnp.zeros_like(token_ref)


def finish(shape, step, rows, terms, held, after, long):
    index, start, width = step
    tile = divisor(width, (1536, 1152, 768, 512, 384, 256, 128))
    aliases = {} if held is None else {len(terms): 0}
    return pl.pallas_call(
        functools.partial(finish_kernel, len(terms)),
        name="finish",
        grid=(width // tile,),
        out_shape=[jax.ShapeDtypeStruct(shape, BF16), jax.ShapeDtypeStruct((8, 128), F32)],
        in_specs=[pl.BlockSpec((rows, tile), lambda j: (0, j))] * len(terms) + [ANY] * (len(aliases) + len(after)),
        out_specs=[
            pl.BlockSpec((rows, tile), lambda j: (index, start // tile + j)),
            pl.BlockSpec((8, 128), lambda j: (0, 0)),
        ],
        input_output_aliases=aliases,
        compiler_params=params(16),
        cost_estimate=cost(12 * rows * width, 6 * rows * width, long),
    )(*terms, *([] if held is None else [held]), *after)


def column_pieces(columns, shares):
    unit, start, pieces = columns // sum(shares), 0, []
    for share in shares:
        pieces.append((start, share * unit))
        start += share * unit
    return pieces


SHARES = ((3, 3), (3, 3), (2, 2, 2))

ORDER = (
    ("f0", "p00", "f1", "p01", "t2", "s00"),
    ("p10", "s01", "f2", "p11-00", "s10"),
    ("p20-01", "s11", "p21-10", "s20", "p22-11+", "g20!"),
    ("s21!", "s22", "g21", "g22"),
)


def local(n_gx, n_gy, hidden, parents, depth_table, weight):
    tree = depth_table.shape[0]
    columns = weight.shape[1]
    block = hidden.shape[0]
    chips = n_gx // 2
    parts = len(SHARES)
    size = block // parts
    place = jnp.stack([lax.axis_index("gx"), lax.axis_index("gy")]).astype(jnp.int32)

    exclusive = n_gy == 4

    def swap(array, distance):
        return lax.ppermute(array, "gy", [(k, k ^ distance) for k in range(n_gy)])

    def later(array, token):
        return lax.optimization_barrier((array, token))[0]

    def take(index, token):
        if not exclusive:
            whole = lax.all_gather(own[index], "gy", axis=0)
            held[index] = [whole[k] for k in range(n_gy)]
        else:
            rows = own[index] if token is None else later(own[index], token)
            held[index] = [own[index], swap(rows, 1), swap(rows, 2)]

    own, held = [hidden[:size]], [None] * parts
    take(0, None)
    onehot = depth_onehot(parents, tree)
    own += embed_own(size, size, parts - 1, place, onehot, depth_table, hidden)

    sibling = [(g, g ^ 1) for g in range(n_gx)]

    def across(ahead):
        return [(g, (g // 2 + ahead) % chips * 2 + g % 2) for g in range(n_gx)]

    out, after = None, own[1:2]
    pieces = [column_pieces(columns, shares) for shares in SHARES]
    products, sums, waiting = {}, {}, {}
    for item in sum(ORDER, ()):
        long = item.endswith("!")
        late = item.endswith("+")
        item = item.rstrip("!+")
        kind, index, piece = item[0], int(item[1]), item[1:3]
        if kind == "f":
            if exclusive:
                given = forward(place, held[index][1], held[index][2], after, long)
                held[index].append(lax.ppermute(given, "gy", [(0, 2), (1, 0), (2, 3), (3, 1)]))
                after = [given]
            if index == 0:
                take(1, after[0] if after else None)
                rows = embed(chips, block, 0, exclusive, place, onehot, depth_table, held[0], after)
                held[0] = [rows]
        if kind == "t":
            take(index, after[0])
        if kind == "p":
            start, width = pieces[index][int(item[2])]
            extra = {}
            if len(item) > 3:
                done = item[4:]
                ending = (int(done[0]) * size, pieces[int(done[0])][int(done[1])][0])
                extra = dict(ending=ending, terms=sums[done], out=out, shape=(block, columns))
            send, keep, *rest = product(chips, exclusive, place, held[index], weight, start, width, after, **extra)
            out = rest[0] if rest else out
            after = [keep]
            if late:
                waiting[piece] = keep, send
            else:
                products[piece] = keep, lax.ppermute(send, "gx", sibling)
        if kind == "s":
            away, stay = pair(chips, *products[piece], after, long)
            sums[piece] = [stay] + [
                lax.ppermute(away[(ahead - 1) * size:ahead * size], "gx", across(ahead)) for ahead in range(1, chips)
            ]
            after = [stay]
        if kind == "g":
            start, width = pieces[index][int(item[2])]
            out, token = finish((block, columns), (index, start, width), size, sums[piece], out, after, long)
            after = [token]
            for name, (keep, send) in waiting.items():
                products[name] = keep, lax.ppermute(later(send, token), "gx", sibling)
            waiting = {}
    return out


def solution(mesh):
    return jax.shard_map(
        functools.partial(local, mesh.shape["gx"], mesh.shape["gy"]),
        mesh=mesh,
        in_specs=(P(("grp", "gy"), "gx"), P("grp"), P(None, "gx"), P("gx", "gy")),
        out_specs=P(("grp", "gx"), "gy"),
        check_vma=False,
    )
```

```python
import functools

import jax
import jax.numpy as jnp
from jax import lax
from jax.experimental import pallas as pl
from jax.experimental.pallas import tpu as pltpu
from jax.sharding import PartitionSpec as P

BF16 = jnp.bfloat16
F32 = jnp.float32
MIB = 1024 * 1024
ANY = pl.BlockSpec(memory_space=pl.ANY)
VMEM = pl.BlockSpec(memory_space=pltpu.VMEM)
SMEM = pl.BlockSpec(memory_space=pltpu.SMEM)


def params(limit):
    return pltpu.CompilerParams(vmem_limit_bytes=limit * MIB)


def cost(flops, accessed, long=False):
    factor = 1000 if long else 8
    return pl.CostEstimate(flops=factor * flops, bytes_accessed=factor * accessed, transcendentals=0)


def divisor(extent, choices):
    for choice in choices:
        if extent % choice == 0:
            return choice
    return extent


def onehot_kernel(tree, parents_ref, onehot_ref):
    lanes = lax.broadcasted_iota(jnp.int32, (tree, tree), 1)
    rows = lax.broadcasted_iota(jnp.int32, (tree, 1), 0)
    firsts = range(0, onehot_ref.shape[0], tree)
    parents = [parents_ref[first:first + tree, :] - first for first in firsts]
    jumps = [(parent == lanes).astype(BF16) for parent in parents]
    depths = [jnp.broadcast_to((parent != rows).astype(F32), (tree, 128)) for parent in parents]
    for level in range((tree - 1).bit_length()):
        depths = [
            depth + jnp.dot(jump, depth.astype(BF16), preferred_element_type=F32)
            for depth, jump in zip(depths, jumps)
        ]
        jumps = [jnp.dot(jump, jump, preferred_element_type=F32).astype(BF16) for jump in jumps]
    for first, depth in zip(firsts, depths):
        onehot_ref[first:first + tree, :] = (depth[:, :1].astype(jnp.int32) == lanes).astype(BF16)


def depth_onehot(parents, tree):
    rows = parents.shape[0]
    return pl.pallas_call(
        functools.partial(onehot_kernel, tree),
        name="onehot",
        out_shape=jax.ShapeDtypeStruct((rows, tree), BF16),
        compiler_params=params(16),
        cost_estimate=cost(48 * rows * tree * tree, 8 * rows * tree),
    )(parents[:, None])


def forward_kernel(place_ref, near_ref, far_ref, *refs):
    out_ref = refs[-1]
    outer = jnp.logical_or(place_ref[1] == 0, place_ref[1] == 3)

    @pl.when(outer)
    def _():
        out_ref[...] = near_ref[...]

    @pl.when(jnp.logical_not(outer))
    def _():
        out_ref[...] = far_ref[...]


def forward(place, near, far, after, long):
    return pl.pallas_call(
        forward_kernel,
        name="forward",
        out_shape=jax.ShapeDtypeStruct(near.shape, near.dtype),
        in_specs=[SMEM, VMEM, VMEM] + [ANY] * len(after),
        out_specs=VMEM,
        compiler_params=params(8),
        cost_estimate=cost(0, 6 * near.size, long),
    )(place, near, far, *after)


def slot_of(dest, chips, gx):
    ahead = lax.rem(dest // 2 - gx // 2 + 2 * chips - 1, chips)
    return jnp.where(lax.rem(gx, 2) == lax.rem(dest, 2), chips, 0) + ahead


def embed_kernel(count, chips, block, first, exclusive, place_ref, onehot_ref, table_ref, *refs):
    rows_ref = refs[-1]
    size = rows_ref.shape[0] // count
    for held in range(count):
        dest = lax.bitwise_xor(place_ref[1], held) if exclusive else held
        slot = slot_of(dest, chips, place_ref[0])
        here = pl.ds(pl.multiple_of(dest * block + first, 16), size)
        looked = jnp.dot(onehot_ref[here, :], table_ref[...], preferred_element_type=F32)
        total = refs[held][...].astype(F32) + looked
        rows_ref[pl.ds(pl.multiple_of(slot * size, 16), size), :] = total.astype(BF16)


def embed(chips, block, first, exclusive, place, onehot, table, held, after):
    count = len(held)
    size, depth = held[0].shape
    tile = divisor(depth, (896, 512, 256, 128))
    piece = pl.BlockSpec((size, tile), lambda j: (0, j))
    return pl.pallas_call(
        functools.partial(embed_kernel, count, chips, block, first, exclusive),
        name="embed",
        grid=(depth // tile,),
        out_shape=jax.ShapeDtypeStruct((count * size, depth), BF16),
        in_specs=[SMEM, pl.BlockSpec(onehot.shape, lambda j: (0, 0)), pl.BlockSpec((table.shape[0], tile), lambda j: (0, j))]
        + [piece] * count + [ANY] * len(after),
        out_specs=pl.BlockSpec((count * size, tile), lambda j: (0, j)),
        compiler_params=params(16),
        cost_estimate=cost(2 * count * size * table.shape[0] * depth, 6 * count * size * depth),
    )(place, onehot, table, *held, *after)


def embed_own_kernel(block, first, place_ref, onehot_ref, table_ref, hidden_ref, *refs):
    start = place_ref[1] * block
    for rows_ref in refs:
        size = rows_ref.shape[0]
        here = pl.ds(pl.multiple_of(start + first, 16), size)
        looked = jnp.dot(onehot_ref[here, :], table_ref[...], preferred_element_type=F32)
        rows_ref[...] = (hidden_ref[first:first + size, :].astype(F32) + looked).astype(BF16)
        first += size


def embed_own(first, size, count, place, onehot, table, hidden):
    block, depth = hidden.shape
    tile = divisor(depth, (896, 512, 256, 128))
    column = lambda j: (0, j)
    return pl.pallas_call(
        functools.partial(embed_own_kernel, block, first),
        name="own",
        grid=(depth // tile,),
        out_shape=[jax.ShapeDtypeStruct((size, depth), BF16)] * count,
        in_specs=[
            SMEM,
            pl.BlockSpec(onehot.shape, lambda j: (0, 0)),
            pl.BlockSpec((table.shape[0], tile), column),
            pl.BlockSpec((block, tile), column),
        ],
        out_specs=[pl.BlockSpec((size, tile), column)] * count,
        compiler_params=params(16),
        cost_estimate=cost(2 * count * size * table.shape[0] * depth, 6 * count * size * depth),
    )(place, onehot, table, hidden)


def gelu_sum(terms):
    total = terms[0].astype(F32)
    for term in terms[1:]:
        total = total + term.astype(F32)
    return jax.nn.gelu(total, approximate=True).astype(BF16)


def product_kernel(start, tile, steps, slots, chips, count, exclusive, ending, place_ref, weight_ref, *refs):
    blocks = refs[:count]
    terms = refs[count:count + ending[3]]
    outs = 2 if not ending[3] else 3
    scratch = len(refs) - (3 if not ending[3] else 7)
    send_ref, keep_ref = refs[scratch - outs:scratch - outs + 2]
    rows, held, arrived = refs[scratch:scratch + 3]
    half = send_ref.shape[0]
    step = pl.program_id(0)

    def fetch(index):
        column = pl.multiple_of(start + index * tile, 128)
        slot = lax.rem(index, slots)
        return pltpu.make_async_copy(weight_ref.at[:, pl.ds(column, tile)], held.at[slot], arrived.at[slot])

    if ending[3]:
        out_ref = refs[scratch - 1]
        term_buffer, out_buffer, term_sems, out_sem = refs[scratch + 3:]
        row, column, width, number = ending
        given = [pltpu.make_async_copy(terms[n], term_buffer.at[n], term_sems.at[n]) for n in range(number)]
        place_out = out_ref.at[row:row + out_buffer.shape[0], column:column + width]
        taken = pltpu.make_async_copy(out_buffer, place_out, out_sem.at[0])

    @pl.when(step == 0)
    def _():
        for index in range(min(slots - 1, steps)):
            fetch(index).start()
        if ending[3]:
            for copy in given:
                copy.start()
        size = rows.shape[0] // count
        for index in range(count):
            first = 0
            if count > 1:
                dest = lax.bitwise_xor(place_ref[1], index) if exclusive else index
                first = pl.multiple_of(slot_of(dest, chips, place_ref[0]) * size, 16)
            rows[pl.ds(first, size), :] = blocks[index][...]

    @pl.when(step + slots - 1 < steps)
    def _():
        fetch(step + slots - 1).start()

    fetch(step).wait()
    out = jnp.dot(rows[...], held[lax.rem(step, slots)], preferred_element_type=F32)
    send_ref[...] = out[:half].astype(BF16)
    keep_ref[...] = out[half:].astype(BF16)

    if ending[3]:
        @pl.when(step == 0)
        def _():
            for copy in given:
                copy.wait()
            part = divisor(width, (512, 384, 256, 128))

            @pl.loop(0, width // part)
            def _(index):
                here = pl.ds(pl.multiple_of(index * part, 128), part)
                out_buffer[:, here] = gelu_sum([term_buffer[n, :, here] for n in range(number)])

            taken.start()

        @pl.when(step == steps - 1)
        def _():
            taken.wait()


def product(chips, exclusive, place, blocks, weight, start, width, after, ending=None, terms=(), out=None, shape=None):
    count = len(blocks)
    height, depth = count * blocks[0].shape[0], blocks[0].shape[1]
    tile = divisor(width, (512, 384, 256, 128))
    slots = 4
    half = jax.ShapeDtypeStruct((height // 2, width), BF16)
    outs = [half, half]
    out_specs = [pl.BlockSpec((height // 2, tile), lambda j: (0, j))] * 2
    scratch = [
        pltpu.VMEM((height, depth), BF16),
        pltpu.VMEM((slots, depth, tile), BF16),
        pltpu.SemaphoreType.DMA((slots,)),
    ]
    operands = [place, weight, *blocks, *terms]
    aliases = {}
    ending = (0, 0, 0, 0) if not terms else (*ending, terms[0].shape[1], len(terms))
    if terms:
        outs.append(jax.ShapeDtypeStruct(shape, BF16))
        out_specs.append(ANY)
        scratch += [
            pltpu.VMEM((len(terms), *terms[0].shape), BF16),
            pltpu.VMEM(terms[0].shape, BF16),
            pltpu.SemaphoreType.DMA((len(terms),)),
            pltpu.SemaphoreType.DMA((1,)),
        ]
        if out is not None:
            aliases = {len(operands): 2}
            operands.append(out)
    operands += after
    return pl.pallas_call(
        functools.partial(product_kernel, start, tile, width // tile, slots, chips, count, exclusive, ending),
        name="product",
        grid=(width // tile,),
        out_shape=outs,
        in_specs=[SMEM, ANY] + [VMEM] * count + [ANY] * (len(operands) - 2 - count),
        out_specs=out_specs,
        scratch_shapes=scratch,
        input_output_aliases=aliases,
        compiler_params=params(40),
        cost_estimate=cost(2 * height * depth * width, 2 * (height * depth + depth * width + height * width)),
    )(*operands)


def pair_kernel(keep_ref, got_ref, *refs):
    away_ref, stay_ref = refs[-2:]
    cut = away_ref.shape[0]
    total = keep_ref[...].astype(F32) + got_ref[...].astype(F32)
    away_ref[...] = total[:cut].astype(BF16)
    stay_ref[...] = total[cut:].astype(BF16)


def pair(chips, keep, got, after, long):
    height, width = keep.shape
    size = height // chips
    tile = width // 2 if width % 256 == 0 else width
    spec = lambda rows: pl.BlockSpec((rows, tile), lambda j: (0, j))
    return pl.pallas_call(
        pair_kernel,
        name="pair",
        grid=(width // tile,),
        out_shape=[jax.ShapeDtypeStruct((height - size, width), BF16), jax.ShapeDtypeStruct((size, width), BF16)],
        in_specs=[spec(height), spec(height)] + [ANY] * len(after),
        out_specs=[spec(height - size), spec(size)],
        compiler_params=params(16),
        cost_estimate=cost(height * width, 6 * height * width, long),
    )(keep, got, *after)


def finish_kernel(count, *refs):
    out_ref, token_ref = refs[-2:]
    out_ref[...] = gelu_sum([refs[index][...] for index in range(count)])
    token_ref[...] = jnp.zeros_like(token_ref)


def finish(shape, step, rows, terms, held, after, long):
    index, start, width = step
    tile = divisor(width, (1536, 1152, 768, 512, 384, 256, 128))
    aliases = {} if held is None else {len(terms): 0}
    return pl.pallas_call(
        functools.partial(finish_kernel, len(terms)),
        name="finish",
        grid=(width // tile,),
        out_shape=[jax.ShapeDtypeStruct(shape, BF16), jax.ShapeDtypeStruct((8, 128), F32)],
        in_specs=[pl.BlockSpec((rows, tile), lambda j: (0, j))] * len(terms) + [ANY] * (len(aliases) + len(after)),
        out_specs=[
            pl.BlockSpec((rows, tile), lambda j: (index, start // tile + j)),
            pl.BlockSpec((8, 128), lambda j: (0, 0)),
        ],
        input_output_aliases=aliases,
        compiler_params=params(16),
        cost_estimate=cost(12 * rows * width, 6 * rows * width, long),
    )(*terms, *([] if held is None else [held]), *after)


def column_pieces(columns, shares):
    unit, start, pieces = columns // sum(shares), 0, []
    for share in shares:
        pieces.append((start, share * unit))
        start += share * unit
    return pieces


SHARES = ((11, 7), (11, 7), (6, 6, 6))

ORDER = (
    ("f0", "p00", "f1", "p01", "t2", "s00"),
    ("p10", "s01", "f2", "p11-00", "s10"),
    ("p20-01", "s11", "p21-10", "s20", "p22-11+", "g20!"),
    ("s21!", "s22", "g21", "g22"),
)


def local(n_gx, n_gy, hidden, parents, depth_table, weight):
    tree = depth_table.shape[0]
    columns = weight.shape[1]
    block = hidden.shape[0]
    chips = n_gx // 2
    parts = len(SHARES)
    size = block // parts
    place = jnp.stack([lax.axis_index("gx"), lax.axis_index("gy")]).astype(jnp.int32)

    exclusive = n_gy == 4

    def swap(array, distance):
        return lax.ppermute(array, "gy", [(k, k ^ distance) for k in range(n_gy)])

    def later(array, token):
        return lax.optimization_barrier((array, token))[0]

    def take(index, token):
        if not exclusive:
            whole = lax.all_gather(own[index], "gy", axis=0)
            held[index] = [whole[k] for k in range(n_gy)]
        else:
            rows = own[index] if token is None else later(own[index], token)
            held[index] = [own[index], swap(rows, 1), swap(rows, 2)]

    own, held = [hidden[:size]], [None] * parts
    take(0, None)
    onehot = depth_onehot(parents, tree)
    own += embed_own(size, size, parts - 1, place, onehot, depth_table, hidden)

    sibling = [(g, g ^ 1) for g in range(n_gx)]

    def across(ahead):
        return [(g, (g // 2 + ahead) % chips * 2 + g % 2) for g in range(n_gx)]

    out, after = None, own[1:2]
    pieces = [column_pieces(columns, shares) for shares in SHARES]
    products, sums, waiting = {}, {}, {}
    for item in sum(ORDER, ()):
        long = item.endswith("!")
        late = item.endswith("+")
        item = item.rstrip("!+")
        kind, index, piece = item[0], int(item[1]), item[1:3]
        if kind == "f":
            if exclusive:
                given = forward(place, held[index][1], held[index][2], after, long)
                held[index].append(lax.ppermute(given, "gy", [(0, 2), (1, 0), (2, 3), (3, 1)]))
                after = [given]
            if index == 0:
                take(1, after[0] if after else None)
                rows = embed(chips, block, 0, exclusive, place, onehot, depth_table, held[0], after)
                held[0] = [rows]
        if kind == "t":
            take(index, after[0])
        if kind == "p":
            start, width = pieces[index][int(item[2])]
            extra = {}
            if len(item) > 3:
                done = item[4:]
                ending = (int(done[0]) * size, pieces[int(done[0])][int(done[1])][0])
                extra = dict(ending=ending, terms=sums[done], out=out, shape=(block, columns))
            send, keep, *rest = product(chips, exclusive, place, held[index], weight, start, width, after, **extra)
            out = rest[0] if rest else out
            after = [keep]
            if late:
                waiting[piece] = keep, send
            else:
                products[piece] = keep, lax.ppermute(send, "gx", sibling)
        if kind == "s":
            away, stay = pair(chips, *products[piece], after, long)
            sums[piece] = [stay] + [
                lax.ppermute(away[(ahead - 1) * size:ahead * size], "gx", across(ahead)) for ahead in range(1, chips)
            ]
            after = [stay]
        if kind == "g":
            start, width = pieces[index][int(item[2])]
            out, token = finish((block, columns), (index, start, width), size, sums[piece], out, after, long)
            after = [token]
            for name, (keep, send) in waiting.items():
                products[name] = keep, lax.ppermute(later(send, token), "gx", sibling)
            waiting = {}
    return out


def solution(mesh):
    return jax.shard_map(
        functools.partial(local, mesh.shape["gx"], mesh.shape["gy"]),
        mesh=mesh,
        in_specs=(P(("grp", "gy"), "gx"), P("grp"), P(None, "gx"), P("gx", "gy")),
        out_specs=P(("grp", "gx"), "gy"),
        check_vma=False,
    )
```

```python
import functools

import jax
import jax.numpy as jnp
from jax import lax
from jax.experimental import pallas as pl
from jax.experimental.pallas import tpu as pltpu
from jax.sharding import PartitionSpec as P

BF16 = jnp.bfloat16
F32 = jnp.float32
MIB = 1024 * 1024
ANY = pl.BlockSpec(memory_space=pl.ANY)
VMEM = pl.BlockSpec(memory_space=pltpu.VMEM)
SMEM = pl.BlockSpec(memory_space=pltpu.SMEM)


def params(limit):
    return pltpu.CompilerParams(vmem_limit_bytes=limit * MIB)


def cost(flops, accessed, long=False):
    factor = 1000 if long else 8
    return pl.CostEstimate(flops=factor * flops, bytes_accessed=factor * accessed, transcendentals=0)


def divisor(extent, choices):
    for choice in choices:
        if extent % choice == 0:
            return choice
    return extent


def onehot_kernel(tree, parents_ref, onehot_ref):
    lanes = lax.broadcasted_iota(jnp.int32, (tree, tree), 1)
    rows = lax.broadcasted_iota(jnp.int32, (tree, 1), 0)
    firsts = range(0, onehot_ref.shape[0], tree)
    parents = [parents_ref[first:first + tree, :] - first for first in firsts]
    jumps = [(parent == lanes).astype(BF16) for parent in parents]
    depths = [jnp.broadcast_to((parent != rows).astype(F32), (tree, 128)) for parent in parents]
    for level in range((tree - 1).bit_length()):
        depths = [
            depth + jnp.dot(jump, depth.astype(BF16), preferred_element_type=F32)
            for depth, jump in zip(depths, jumps)
        ]
        jumps = [jnp.dot(jump, jump, preferred_element_type=F32).astype(BF16) for jump in jumps]
    for first, depth in zip(firsts, depths):
        onehot_ref[first:first + tree, :] = (depth[:, :1].astype(jnp.int32) == lanes).astype(BF16)


def depth_onehot(parents, tree):
    rows = parents.shape[0]
    return pl.pallas_call(
        functools.partial(onehot_kernel, tree),
        name="onehot",
        out_shape=jax.ShapeDtypeStruct((rows, tree), BF16),
        compiler_params=params(16),
        cost_estimate=cost(48 * rows * tree * tree, 8 * rows * tree),
    )(parents[:, None])


def forward_kernel(place_ref, near_ref, far_ref, *refs):
    out_ref = refs[-1]
    outer = jnp.logical_or(place_ref[1] == 0, place_ref[1] == 3)

    @pl.when(outer)
    def _():
        out_ref[...] = near_ref[...]

    @pl.when(jnp.logical_not(outer))
    def _():
        out_ref[...] = far_ref[...]


def forward(place, near, far, after, long):
    return pl.pallas_call(
        forward_kernel,
        name="forward",
        out_shape=jax.ShapeDtypeStruct(near.shape, near.dtype),
        in_specs=[SMEM, VMEM, VMEM] + [ANY] * len(after),
        out_specs=VMEM,
        compiler_params=params(8),
        cost_estimate=cost(0, 6 * near.size, long),
    )(place, near, far, *after)


def slot_of(dest, chips, gx):
    ahead = lax.rem(dest // 2 - gx // 2 + 2 * chips - 1, chips)
    return jnp.where(lax.rem(gx, 2) == lax.rem(dest, 2), chips, 0) + ahead


def look_kernel(count, chips, block, first, exclusive, place_ref, onehot_ref, table_ref, *refs):
    looked_ref = refs[-1]
    size = looked_ref.shape[0] // count
    for dest in range(count):
        here = pl.ds(dest * block + first, size)
        looked = jnp.dot(onehot_ref[here, :], table_ref[...], preferred_element_type=F32)
        slot = pl.multiple_of(slot_of(dest, chips, place_ref[0]) * size, 16)
        looked_ref[pl.ds(slot, size), :] = looked.astype(BF16)


def look(chips, count, block, first, size, exclusive, place, onehot, table, after):
    depth = table.shape[1]
    tile = divisor(depth, (896, 512, 256, 128))
    return pl.pallas_call(
        functools.partial(look_kernel, count, chips, block, first, exclusive),
        name="look",
        grid=(depth // tile,),
        out_shape=jax.ShapeDtypeStruct((count * size, depth), BF16),
        in_specs=[SMEM, pl.BlockSpec(onehot.shape, lambda j: (0, 0)), pl.BlockSpec((table.shape[0], tile), lambda j: (0, j))]
        + [ANY] * len(after),
        out_specs=pl.BlockSpec((count * size, tile), lambda j: (0, j)),
        compiler_params=params(16),
        cost_estimate=cost(2 * count * size * table.shape[0] * depth, 4 * count * size * depth),
    )(place, onehot, table, *after)


def arrange_kernel(count, chips, exclusive, added, place_ref, *refs):
    rows_ref = refs[-1]
    size = rows_ref.shape[0] // count
    for held in range(count):
        dest = lax.bitwise_xor(place_ref[1], held) if exclusive else held
        here = pl.ds(pl.multiple_of(slot_of(dest, chips, place_ref[0]) * size, 16), size)
        if added:
            rows_ref[here, :] = (refs[held][...].astype(F32) + refs[count][here, :].astype(F32)).astype(BF16)
        else:
            rows_ref[here, :] = refs[held][...]


def arrange(chips, exclusive, place, held, looked, after):
    count = len(held)
    size, depth = held[0].shape
    added = [] if looked is None else [looked]
    return pl.pallas_call(
        functools.partial(arrange_kernel, count, chips, exclusive, bool(added)),
        name="arrange",
        out_shape=jax.ShapeDtypeStruct((count * size, depth), BF16),
        in_specs=[SMEM] + [VMEM] * (count + len(added)) + [ANY] * len(after),
        out_specs=VMEM,
        compiler_params=params(16),
        cost_estimate=cost(count * size * depth, 6 * count * size * depth),
    )(place, *held, *added, *after)


def embed_own_kernel(block, first, place_ref, onehot_ref, table_ref, hidden_ref, *refs):
    start = place_ref[1] * block
    for rows_ref in refs:
        size = rows_ref.shape[0]
        here = pl.ds(pl.multiple_of(start + first, 16), size)
        looked = jnp.dot(onehot_ref[here, :], table_ref[...], preferred_element_type=F32)
        rows_ref[...] = (hidden_ref[first:first + size, :].astype(F32) + looked).astype(BF16)
        first += size


def embed_own(first, size, count, place, onehot, table, hidden):
    block, depth = hidden.shape
    tile = divisor(depth, (896, 512, 256, 128))
    column = lambda j: (0, j)
    return pl.pallas_call(
        functools.partial(embed_own_kernel, block, first),
        name="own",
        grid=(depth // tile,),
        out_shape=[jax.ShapeDtypeStruct((size, depth), BF16)] * count,
        in_specs=[
            SMEM,
            pl.BlockSpec(onehot.shape, lambda j: (0, 0)),
            pl.BlockSpec((table.shape[0], tile), column),
            pl.BlockSpec((block, tile), column),
        ],
        out_specs=[pl.BlockSpec((size, tile), column)] * count,
        compiler_params=params(16),
        cost_estimate=cost(2 * count * size * table.shape[0] * depth, 6 * count * size * depth),
    )(place, onehot, table, hidden)


def gelu_sum(terms):
    total = terms[0].astype(F32)
    for term in terms[1:]:
        total = total + term.astype(F32)
    return jax.nn.gelu(total, approximate=True).astype(BF16)


def product_kernel(start, tile, steps, slots, ending, rows_ref, weight_ref, *refs):
    terms = refs[:ending[3]]
    outs = 2 if not ending[3] else 3
    scratch = len(refs) - (2 if not ending[3] else 6)
    send_ref, keep_ref = refs[scratch - outs:scratch - outs + 2]
    held, arrived = refs[scratch:scratch + 2]
    half = send_ref.shape[0]
    step = pl.program_id(0)

    def fetch(index):
        column = pl.multiple_of(start + index * tile, 128)
        slot = lax.rem(index, slots)
        return pltpu.make_async_copy(weight_ref.at[:, pl.ds(column, tile)], held.at[slot], arrived.at[slot])

    if ending[3]:
        out_ref = refs[scratch - 1]
        term_buffer, out_buffer, term_sems, out_sem = refs[scratch + 2:]
        row, column, width, number = ending
        given = [pltpu.make_async_copy(terms[n], term_buffer.at[n], term_sems.at[n]) for n in range(number)]
        place_out = out_ref.at[row:row + out_buffer.shape[0], column:column + width]
        taken = pltpu.make_async_copy(out_buffer, place_out, out_sem.at[0])

    @pl.when(step == 0)
    def _():
        for index in range(min(slots - 1, steps)):
            fetch(index).start()
        if ending[3]:
            for copy in given:
                copy.start()

    @pl.when(step + slots - 1 < steps)
    def _():
        fetch(step + slots - 1).start()

    fetch(step).wait()
    out = jnp.dot(rows_ref[...], held[lax.rem(step, slots)], preferred_element_type=F32)
    send_ref[...] = out[:half].astype(BF16)
    keep_ref[...] = out[half:].astype(BF16)

    if ending[3]:
        @pl.when(step == 0)
        def _():
            for copy in given:
                copy.wait()
            part = divisor(width, (512, 384, 256, 128))

            @pl.loop(0, width // part)
            def _(index):
                here = pl.ds(pl.multiple_of(index * part, 128), part)
                out_buffer[:, here] = gelu_sum([term_buffer[n, :, here] for n in range(number)])

            taken.start()

        @pl.when(step == steps - 1)
        def _():
            taken.wait()


def product(rows, weight, start, width, after, ending=None, terms=(), out=None, shape=None):
    height, depth = rows.shape
    tile = divisor(width, (512, 384, 256, 128))
    slots = 4
    half = jax.ShapeDtypeStruct((height // 2, width), BF16)
    outs = [half, half]
    out_specs = [pl.BlockSpec((height // 2, tile), lambda j: (0, j))] * 2
    scratch = [
        pltpu.VMEM((slots, depth, tile), BF16),
        pltpu.SemaphoreType.DMA((slots,)),
    ]
    operands = [rows, weight, *terms]
    aliases = {}
    ending = (0, 0, 0, 0) if not terms else (*ending, terms[0].shape[1], len(terms))
    if terms:
        outs.append(jax.ShapeDtypeStruct(shape, BF16))
        out_specs.append(ANY)
        scratch += [
            pltpu.VMEM((len(terms), *terms[0].shape), BF16),
            pltpu.VMEM(terms[0].shape, BF16),
            pltpu.SemaphoreType.DMA((len(terms),)),
            pltpu.SemaphoreType.DMA((1,)),
        ]
        if out is not None:
            aliases = {len(operands): 2}
            operands.append(out)
    operands += after
    return pl.pallas_call(
        functools.partial(product_kernel, start, tile, width // tile, slots, ending),
        name="product",
        grid=(width // tile,),
        out_shape=outs,
        in_specs=[VMEM] + [ANY] * (len(operands) - 1),
        out_specs=out_specs,
        scratch_shapes=scratch,
        input_output_aliases=aliases,
        compiler_params=params(40),
        cost_estimate=cost(2 * height * depth * width, 2 * (height * depth + depth * width + height * width)),
    )(*operands)


def pair_kernel(keep_ref, got_ref, *refs):
    away_ref, stay_ref = refs[-2:]
    cut = away_ref.shape[0]
    total = keep_ref[...].astype(F32) + got_ref[...].astype(F32)
    away_ref[...] = total[:cut].astype(BF16)
    stay_ref[...] = total[cut:].astype(BF16)


def pair(chips, keep, got, after, long):
    height, width = keep.shape
    size = height // chips
    tile = width // 2 if width % 256 == 0 else width
    spec = lambda rows: pl.BlockSpec((rows, tile), lambda j: (0, j))
    return pl.pallas_call(
        pair_kernel,
        name="pair",
        grid=(width // tile,),
        out_shape=[jax.ShapeDtypeStruct((height - size, width), BF16), jax.ShapeDtypeStruct((size, width), BF16)],
        in_specs=[spec(height), spec(height)] + [ANY] * len(after),
        out_specs=[spec(height - size), spec(size)],
        compiler_params=params(16),
        cost_estimate=cost(height * width, 6 * height * width, long),
    )(keep, got, *after)


def finish_kernel(count, *refs):
    out_ref, token_ref = refs[-2:]
    out_ref[...] = gelu_sum([refs[index][...] for index in range(count)])
    token_ref[...] = jnp.zeros_like(token_ref)


def finish(shape, step, rows, terms, held, after, long):
    index, start, width = step
    tile = divisor(width, (1536, 1152, 768, 512, 384, 256, 128))
    aliases = {} if held is None else {len(terms): 0}
    return pl.pallas_call(
        functools.partial(finish_kernel, len(terms)),
        name="finish",
        grid=(width // tile,),
        out_shape=[jax.ShapeDtypeStruct(shape, BF16), jax.ShapeDtypeStruct((8, 128), F32)],
        in_specs=[pl.BlockSpec((rows, tile), lambda j: (0, j))] * len(terms) + [ANY] * (len(aliases) + len(after)),
        out_specs=[
            pl.BlockSpec((rows, tile), lambda j: (index, start // tile + j)),
            pl.BlockSpec((8, 128), lambda j: (0, 0)),
        ],
        input_output_aliases=aliases,
        compiler_params=params(16),
        cost_estimate=cost(12 * rows * width, 6 * rows * width, long),
    )(*terms, *([] if held is None else [held]), *after)


def column_pieces(columns, shares):
    unit, start, pieces = columns // sum(shares), 0, []
    for share in shares:
        pieces.append((start, share * unit))
        start += share * unit
    return pieces


SHARES = ((11, 7), (11, 7), (6, 6, 6))

ORDER = (
    ("f0", "a0", "p00", "f1", "p01", "t2", "s00"),
    ("a1", "p10", "s01", "f2", "p11-00", "s10"),
    ("a2", "p20-01", "s11", "p21-10", "s20", "p22-11+", "g20!"),
    ("s21!", "s22", "g21", "g22"),
)


def local(n_gx, n_gy, hidden, parents, depth_table, weight):
    tree = depth_table.shape[0]
    columns = weight.shape[1]
    block = hidden.shape[0]
    chips = n_gx // 2
    parts = len(SHARES)
    size = block // parts
    place = jnp.stack([lax.axis_index("gx"), lax.axis_index("gy")]).astype(jnp.int32)

    exclusive = n_gy == 4

    def swap(array, distance):
        return lax.ppermute(array, "gy", [(k, k ^ distance) for k in range(n_gy)])

    def later(array, token):
        return lax.optimization_barrier((array, token))[0]

    def take(index, token):
        if not exclusive:
            whole = lax.all_gather(own[index], "gy", axis=0)
            held[index] = [whole[k] for k in range(n_gy)]
        else:
            rows = own[index] if token is None else later(own[index], token)
            held[index] = [own[index], None if index == 1 else swap(rows, 1), swap(rows, 2)]

    own, held = [hidden[:size]], [None] * parts
    take(0, None)
    onehot = depth_onehot(parents, tree)
    own += embed_own(size, size, parts - 1, place, onehot, depth_table, hidden)

    sibling = [(g, g ^ 1) for g in range(n_gx)]

    def across(ahead):
        return [(g, (g // 2 + ahead) % chips * 2 + g % 2) for g in range(n_gx)]

    out, after = None, own[1:2]
    pieces = [column_pieces(columns, shares) for shares in SHARES]
    products, sums, waiting = {}, {}, {}
    for item in sum(ORDER, ()):
        long = item.endswith("!")
        late = item.endswith("+")
        item = item.rstrip("!+")
        kind, index, piece = item[0], int(item[1]), item[1:3]
        if kind == "f":
            if exclusive:
                given = forward(place, held[index][1], held[index][2], after, long)
                held[index].append(lax.ppermute(given, "gy", [(0, 2), (1, 0), (2, 3), (3, 1)]))
                after = [given]
            if index == 0:
                take(1, after[0] if after else None)
                looked = look(chips, n_gx, block, 0, size, exclusive, place, onehot, depth_table, after)
        if kind == "t":
            take(index, after[0])
        if kind == "a":
            rows = arrange(chips, exclusive, place, held[index], None if index else looked, after)
            after = [rows]
            if exclusive and index == 0:
                held[1][1] = swap(later(own[1], rows), 1)
        if kind == "p":
            start, width = pieces[index][int(item[2])]
            extra = {}
            if len(item) > 3:
                done = item[4:]
                ending = (int(done[0]) * size, pieces[int(done[0])][int(done[1])][0])
                extra = dict(ending=ending, terms=sums[done], out=out, shape=(block, columns))
            send, keep, *rest = product(rows, weight, start, width, after, **extra)
            out = rest[0] if rest else out
            after = [keep]
            if late:
                waiting[piece] = keep, send
            else:
                products[piece] = keep, lax.ppermute(send, "gx", sibling)
        if kind == "s":
            away, stay = pair(chips, *products[piece], after, long)
            sums[piece] = [stay] + [
                lax.ppermute(away[(ahead - 1) * size:ahead * size], "gx", across(ahead)) for ahead in range(1, chips)
            ]
            after = [stay]
        if kind == "g":
            start, width = pieces[index][int(item[2])]
            out, token = finish((block, columns), (index, start, width), size, sums[piece], out, after, long)
            after = [token]
            for name, (keep, send) in waiting.items():
                products[name] = keep, lax.ppermute(later(send, token), "gx", sibling)
            waiting = {}
    return out


def solution(mesh):
    return jax.shard_map(
        functools.partial(local, mesh.shape["gx"], mesh.shape["gy"]),
        mesh=mesh,
        in_specs=(P(("grp", "gy"), "gx"), P("grp"), P(None, "gx"), P("gx", "gy")),
        out_specs=P(("grp", "gx"), "gy"),
        check_vma=False,
    )
```

```python
import functools

import jax
import jax.numpy as jnp
from jax import lax
from jax.experimental import pallas as pl
from jax.experimental.pallas import tpu as pltpu
from jax.sharding import PartitionSpec as P

BF16 = jnp.bfloat16
F32 = jnp.float32
MIB = 1024 * 1024
ANY = pl.BlockSpec(memory_space=pl.ANY)
VMEM = pl.BlockSpec(memory_space=pltpu.VMEM)
SMEM = pl.BlockSpec(memory_space=pltpu.SMEM)


def params(limit):
    return pltpu.CompilerParams(vmem_limit_bytes=limit * MIB)


def cost(flops, accessed, long=False):
    factor = 1000 if long else 8
    return pl.CostEstimate(flops=factor * flops, bytes_accessed=factor * accessed, transcendentals=0)


def divisor(extent, choices):
    for choice in choices:
        if extent % choice == 0:
            return choice
    return extent


def onehot_kernel(tree, parents_ref, onehot_ref):
    lanes = lax.broadcasted_iota(jnp.int32, (tree, tree), 1)
    rows = lax.broadcasted_iota(jnp.int32, (tree, 1), 0)
    firsts = range(0, onehot_ref.shape[0], tree)
    parents = [parents_ref[first:first + tree, :] - first for first in firsts]
    jumps = [(parent == lanes).astype(BF16) for parent in parents]
    depths = [jnp.broadcast_to((parent != rows).astype(F32), (tree, 128)) for parent in parents]
    for level in range((tree - 1).bit_length()):
        depths = [
            depth + jnp.dot(jump, depth.astype(BF16), preferred_element_type=F32)
            for depth, jump in zip(depths, jumps)
        ]
        jumps = [jnp.dot(jump, jump, preferred_element_type=F32).astype(BF16) for jump in jumps]
    for first, depth in zip(firsts, depths):
        onehot_ref[first:first + tree, :] = (depth[:, :1].astype(jnp.int32) == lanes).astype(BF16)


def depth_onehot(parents, tree):
    rows = parents.shape[0]
    return pl.pallas_call(
        functools.partial(onehot_kernel, tree),
        name="onehot",
        out_shape=jax.ShapeDtypeStruct((rows, tree), BF16),
        compiler_params=params(16),
        cost_estimate=cost(48 * rows * tree * tree, 8 * rows * tree),
    )(parents[:, None])


def forward_kernel(place_ref, near_ref, far_ref, *refs):
    out_ref = refs[-1]
    outer = jnp.logical_or(place_ref[1] == 0, place_ref[1] == 3)

    @pl.when(outer)
    def _():
        out_ref[...] = near_ref[...]

    @pl.when(jnp.logical_not(outer))
    def _():
        out_ref[...] = far_ref[...]


def forward(place, near, far, after, long):
    return pl.pallas_call(
        forward_kernel,
        name="forward",
        out_shape=jax.ShapeDtypeStruct(near.shape, near.dtype),
        in_specs=[SMEM, VMEM, VMEM] + [ANY] * len(after),
        out_specs=VMEM,
        compiler_params=params(8),
        cost_estimate=cost(0, 6 * near.size, long),
    )(place, near, far, *after)


def slot_of(dest, chips, gx):
    ahead = lax.rem(dest // 2 - gx // 2 + 2 * chips - 1, chips)
    return jnp.where(lax.rem(gx, 2) == lax.rem(dest, 2), chips, 0) + ahead


def look_kernel(count, chips, block, first, exclusive, place_ref, onehot_ref, table_ref, *refs):
    looked_ref = refs[-1]
    size = looked_ref.shape[0] // count
    for dest in range(count):
        here = pl.ds(dest * block + first, size)
        looked = jnp.dot(onehot_ref[here, :], table_ref[...], preferred_element_type=F32)
        slot = pl.multiple_of(slot_of(dest, chips, place_ref[0]) * size, 16)
        looked_ref[pl.ds(slot, size), :] = looked.astype(BF16)


def look(chips, count, block, first, size, exclusive, place, onehot, table, after):
    depth = table.shape[1]
    tile = divisor(depth, (896, 512, 256, 128))
    return pl.pallas_call(
        functools.partial(look_kernel, count, chips, block, first, exclusive),
        name="look",
        grid=(depth // tile,),
        out_shape=jax.ShapeDtypeStruct((count * size, depth), BF16),
        in_specs=[SMEM, pl.BlockSpec(onehot.shape, lambda j: (0, 0)), pl.BlockSpec((table.shape[0], tile), lambda j: (0, j))]
        + [ANY] * len(after),
        out_specs=pl.BlockSpec((count * size, tile), lambda j: (0, j)),
        compiler_params=params(16),
        cost_estimate=cost(2 * count * size * table.shape[0] * depth, 4 * count * size * depth),
    )(place, onehot, table, *after)


def arrange_kernel(count, chips, exclusive, added, place_ref, *refs):
    rows_ref = refs[-1]
    size = rows_ref.shape[0] // count
    for held in range(count):
        dest = lax.bitwise_xor(place_ref[1], held) if exclusive else held
        here = pl.ds(pl.multiple_of(slot_of(dest, chips, place_ref[0]) * size, 16), size)
        if added:
            rows_ref[here, :] = (refs[held][...].astype(F32) + refs[count][here, :].astype(F32)).astype(BF16)
        else:
            rows_ref[here, :] = refs[held][...]


def arrange(chips, exclusive, place, held, looked, after):
    count = len(held)
    size, depth = held[0].shape
    added = [] if looked is None else [looked]
    return pl.pallas_call(
        functools.partial(arrange_kernel, count, chips, exclusive, bool(added)),
        name="arrange",
        out_shape=jax.ShapeDtypeStruct((count * size, depth), BF16),
        in_specs=[SMEM] + [VMEM] * (count + len(added)) + [ANY] * len(after),
        out_specs=VMEM,
        compiler_params=params(16),
        cost_estimate=cost(count * size * depth, 6 * count * size * depth),
    )(place, *held, *added, *after)


def embed_own_kernel(block, first, place_ref, onehot_ref, table_ref, hidden_ref, *refs):
    start = place_ref[1] * block
    for rows_ref in refs:
        size = rows_ref.shape[0]
        here = pl.ds(pl.multiple_of(start + first, 16), size)
        looked = jnp.dot(onehot_ref[here, :], table_ref[...], preferred_element_type=F32)
        rows_ref[...] = (hidden_ref[first:first + size, :].astype(F32) + looked).astype(BF16)
        first += size


def embed_own(sizes, place, onehot, table, hidden):
    block, depth = hidden.shape
    tile = divisor(depth, (896, 512, 256, 128))
    column = lambda j: (0, j)
    return pl.pallas_call(
        functools.partial(embed_own_kernel, block, block - sum(sizes)),
        name="own",
        grid=(depth // tile,),
        out_shape=[jax.ShapeDtypeStruct((size, depth), BF16) for size in sizes],
        in_specs=[
            SMEM,
            pl.BlockSpec(onehot.shape, lambda j: (0, 0)),
            pl.BlockSpec((table.shape[0], tile), column),
            pl.BlockSpec((block, tile), column),
        ],
        out_specs=[pl.BlockSpec((size, tile), column) for size in sizes],
        compiler_params=params(16),
        cost_estimate=cost(2 * sum(sizes) * table.shape[0] * depth, 6 * sum(sizes) * depth),
    )(place, onehot, table, hidden)


def gelu_sum(terms):
    total = terms[0].astype(F32)
    for term in terms[1:]:
        total = total + term.astype(F32)
    return jax.nn.gelu(total, approximate=True).astype(BF16)


def product_kernel(start, tile, steps, slots, ending, rows_ref, lead_ref, weight_ref, *refs):
    terms = refs[:ending[3]]
    outs = 2 if not ending[3] else 3
    scratch = len(refs) - (2 if not ending[3] else 6)
    send_ref, keep_ref = refs[scratch - outs:scratch - outs + 2]
    held, arrived = refs[scratch:scratch + 2]
    half = send_ref.shape[0]
    step = pl.program_id(0)

    def fetch(index):
        column = pl.multiple_of(start + index * tile, 128)
        slot = lax.rem(index, slots)
        return pltpu.make_async_copy(weight_ref.at[:, pl.ds(column, tile)], held.at[slot], arrived.at[slot])

    if ending[3]:
        out_ref = refs[scratch - 1]
        term_buffer, out_buffer, term_sems, out_sem = refs[scratch + 2:]
        row, column, width, number = ending
        given = [pltpu.make_async_copy(terms[n], term_buffer.at[n], term_sems.at[n]) for n in range(number)]
        place_out = out_ref.at[row:row + out_buffer.shape[0], column:column + width]
        taken = pltpu.make_async_copy(out_buffer, place_out, out_sem.at[0])

    @pl.when(step == 0)
    def _():
        for index in range(1, min(slots - 1, steps)):
            fetch(index).start()
        if ending[3]:
            for copy in given:
                copy.start()

    @pl.when(step + slots - 1 < steps)
    def _():
        fetch(step + slots - 1).start()

    def multiply(tile_ref):
        out = jnp.dot(rows_ref[...], tile_ref[...], preferred_element_type=F32)
        send_ref[...] = out[:half].astype(BF16)
        keep_ref[...] = out[half:].astype(BF16)

    @pl.when(step == 0)
    def _():
        multiply(lead_ref)

    @pl.when(step > 0)
    def _():
        fetch(step).wait()
        multiply(held.at[lax.rem(step, slots)])

    if ending[3]:
        @pl.when(step == 0)
        def _():
            for copy in given:
                copy.wait()
            part = divisor(width, (512, 384, 256, 128))

            @pl.loop(0, width // part)
            def _(index):
                here = pl.ds(pl.multiple_of(index * part, 128), part)
                out_buffer[:, here] = gelu_sum([term_buffer[n, :, here] for n in range(number)])

            taken.start()

        @pl.when(step == steps - 1)
        def _():
            taken.wait()


def product(rows, weight, start, width, after, ending=None, terms=(), out=None, shape=None):
    height, depth = rows.shape
    tile = divisor(width, (512, 384, 256, 128))
    slots = 4
    half = jax.ShapeDtypeStruct((height // 2, width), BF16)
    outs = [half, half]
    out_specs = [pl.BlockSpec((height // 2, tile), lambda j: (0, j))] * 2
    scratch = [
        pltpu.VMEM((slots, depth, tile), BF16),
        pltpu.SemaphoreType.DMA((slots,)),
    ]
    operands = [rows, weight[:, start:start + tile], weight, *terms]
    aliases = {}
    ending = (0, 0, 0, 0) if not terms else (*ending, terms[0].shape[1], len(terms))
    if terms:
        outs.append(jax.ShapeDtypeStruct(shape, BF16))
        out_specs.append(ANY)
        scratch += [
            pltpu.VMEM((len(terms), *terms[0].shape), BF16),
            pltpu.VMEM(terms[0].shape, BF16),
            pltpu.SemaphoreType.DMA((len(terms),)),
            pltpu.SemaphoreType.DMA((1,)),
        ]
        if out is not None:
            aliases = {len(operands): 2}
            operands.append(out)
    operands += after
    return pl.pallas_call(
        functools.partial(product_kernel, start, tile, width // tile, slots, ending),
        name="product",
        grid=(width // tile,),
        out_shape=outs,
        in_specs=[VMEM] * 2 + [ANY] * (len(operands) - 2),
        out_specs=out_specs,
        scratch_shapes=scratch,
        input_output_aliases=aliases,
        compiler_params=params(24),
        cost_estimate=cost(2 * height * depth * width, 2 * (height * depth + depth * width + height * width)),
    )(*operands)


def pair_kernel(keep_ref, got_ref, *refs):
    away_ref, stay_ref = refs[-2:]
    cut = away_ref.shape[0]
    total = keep_ref[...].astype(F32) + got_ref[...].astype(F32)
    away_ref[...] = total[:cut].astype(BF16)
    stay_ref[...] = total[cut:].astype(BF16)


def pair(chips, keep, got, after, long):
    height, width = keep.shape
    size = height // chips
    tile = width // 2 if width % 256 == 0 else width
    spec = lambda rows: pl.BlockSpec((rows, tile), lambda j: (0, j))
    return pl.pallas_call(
        pair_kernel,
        name="pair",
        grid=(width // tile,),
        out_shape=[jax.ShapeDtypeStruct((height - size, width), BF16), jax.ShapeDtypeStruct((size, width), BF16)],
        in_specs=[spec(height), spec(height)] + [ANY] * len(after),
        out_specs=[spec(height - size), spec(size)],
        compiler_params=params(16),
        cost_estimate=cost(height * width, 6 * height * width, long),
    )(keep, got, *after)


def finish_kernel(count, *refs):
    out_ref, token_ref = refs[-2:]
    out_ref[...] = gelu_sum([refs[index][...] for index in range(count)])
    token_ref[...] = jnp.zeros_like(token_ref)


def finish(shape, step, rows, terms, held, after, long):
    index, start, width = step
    tile = divisor(width, (1536, 1152, 768, 512, 384, 256, 128))
    aliases = {} if held is None else {len(terms): 0}
    return pl.pallas_call(
        functools.partial(finish_kernel, len(terms)),
        name="finish",
        grid=(width // tile,),
        out_shape=[jax.ShapeDtypeStruct(shape, BF16), jax.ShapeDtypeStruct((8, 128), F32)],
        in_specs=[pl.BlockSpec((rows, tile), lambda j: (0, j))] * len(terms) + [ANY] * (len(aliases) + len(after)),
        out_specs=[
            pl.BlockSpec((rows, tile), lambda j: (index, start // tile + j)),
            pl.BlockSpec((8, 128), lambda j: (0, 0)),
        ],
        input_output_aliases=aliases,
        compiler_params=params(16),
        cost_estimate=cost(12 * rows * width, 6 * rows * width, long),
    )(*terms, *([] if held is None else [held]), *after)


def column_pieces(columns, shares):
    unit, start, pieces = columns // sum(shares), 0, []
    for share in shares:
        pieces.append((start, share * unit))
        start += share * unit
    return pieces


SHARES = ((9, 9), (6, 6, 6), (6, 6, 6))


def chunk_sizes(block):
    if block % 192 == 0:
        return [block // 4, block * 5 // 12, block // 3]
    return [block // 3] * 3


ORDER = (
    ("f0", "a0", "p00", "p01", "s00", "f1", "s01"),
    ("a1", "t2", "p10", "p11-00", "f2", "s10", "p12-01", "s11"),
    ("a2", "p20-10", "s12", "p21-11", "s20", "p22-12+", "g20!"),
    ("s21!", "s22", "g21", "g22"),
)


def local(n_gx, n_gy, hidden, parents, depth_table, weight):
    tree = depth_table.shape[0]
    columns = weight.shape[1]
    block = hidden.shape[0]
    chips = n_gx // 2
    sizes = chunk_sizes(block)
    firsts = [sum(sizes[:index]) for index in range(len(sizes))]
    parts = len(sizes)
    place = jnp.stack([lax.axis_index("gx"), lax.axis_index("gy")]).astype(jnp.int32)

    exclusive = n_gy == 4

    def swap(array, distance):
        return lax.ppermute(array, "gy", [(k, k ^ distance) for k in range(n_gy)])

    def later(array, token):
        return lax.optimization_barrier((array, token))[0]

    def take(index, token):
        if not exclusive:
            whole = lax.all_gather(own[index], "gy", axis=0)
            held[index] = [whole[k] for k in range(n_gy)]
        else:
            rows = own[index] if token is None else later(own[index], token)
            held[index] = [own[index], None if index == 1 else swap(rows, 1), swap(rows, 2)]

    own, held = [hidden[:sizes[0]]], [None] * parts
    take(0, None)
    onehot = depth_onehot(parents, tree)
    own += embed_own(sizes[1:], place, onehot, depth_table, hidden)

    sibling = [(g, g ^ 1) for g in range(n_gx)]

    def across(ahead):
        return [(g, (g // 2 + ahead) % chips * 2 + g % 2) for g in range(n_gx)]

    out, after = None, own[1:2]
    pieces = [column_pieces(columns, shares) for shares in SHARES]
    products, sums, waiting = {}, {}, {}
    for item in sum(ORDER, ()):
        long = item.endswith("!")
        late = item.endswith("+")
        item = item.rstrip("!+")
        kind, index, piece = item[0], int(item[1]), item[1:3]
        if kind == "f":
            if exclusive:
                given = forward(place, held[index][1], held[index][2], after, long)
                held[index].append(lax.ppermute(given, "gy", [(0, 2), (1, 0), (2, 3), (3, 1)]))
                after = [given]
            if index == 0:
                take(1, after[0] if after else None)
                looked = look(chips, n_gx, block, 0, sizes[0], exclusive, place, onehot, depth_table, after)
        if kind == "t":
            take(index, after[0])
        if kind == "a":
            rows = arrange(chips, exclusive, place, held[index], None if index else looked, after)
            after = [rows]
            if exclusive and index == 0:
                held[1][1] = swap(later(own[1], rows), 1)
        if kind == "p":
            start, width = pieces[index][int(item[2])]
            extra = {}
            if len(item) > 3:
                done = item[4:]
                ending = (firsts[int(done[0])], pieces[int(done[0])][int(done[1])][0])
                extra = dict(ending=ending, terms=sums[done], out=out, shape=(block, columns))
            send, keep, *rest = product(rows, weight, start, width, after, **extra)
            out = rest[0] if rest else out
            after = [keep]
            if late:
                waiting[piece] = keep, send
            else:
                products[piece] = keep, lax.ppermute(send, "gx", sibling)
        if kind == "s":
            away, stay = pair(chips, *products[piece], after, long)
            size = sizes[index]
            sums[piece] = [stay] + [
                lax.ppermute(away[(ahead - 1) * size:ahead * size], "gx", across(ahead)) for ahead in range(1, chips)
            ]
            after = [stay]
        if kind == "g":
            start, width = pieces[index][int(item[2])]
            out, token = finish((block, columns), (firsts[index] // sizes[index], start, width), sizes[index], sums[piece], out, after, long)
            after = [token]
            for name, (keep, send) in waiting.items():
                products[name] = keep, lax.ppermute(later(send, token), "gx", sibling)
            waiting = {}
    return out


def solution(mesh):
    return jax.shard_map(
        functools.partial(local, mesh.shape["gx"], mesh.shape["gy"]),
        mesh=mesh,
        in_specs=(P(("grp", "gy"), "gx"), P("grp"), P(None, "gx"), P("gx", "gy")),
        out_specs=P(("grp", "gx"), "gy"),
        check_vma=False,
    )
```

```python
import functools

import jax
import jax.numpy as jnp
from jax import lax
from jax.experimental import pallas as pl
from jax.experimental.pallas import tpu as pltpu
from jax.sharding import PartitionSpec as P

BF16 = jnp.bfloat16
F32 = jnp.float32
MIB = 1024 * 1024
ANY = pl.BlockSpec(memory_space=pl.ANY)
VMEM = pl.BlockSpec(memory_space=pltpu.VMEM)
SMEM = pl.BlockSpec(memory_space=pltpu.SMEM)


def params(limit):
    return pltpu.CompilerParams(vmem_limit_bytes=limit * MIB)


def cost(flops, accessed, long=False):
    factor = 1000 if long else 8
    return pl.CostEstimate(flops=factor * flops, bytes_accessed=factor * accessed, transcendentals=0)


def divisor(extent, choices):
    for choice in choices:
        if extent % choice == 0:
            return choice
    return extent


def onehot_kernel(tree, parents_ref, onehot_ref):
    lanes = lax.broadcasted_iota(jnp.int32, (tree, tree), 1)
    rows = lax.broadcasted_iota(jnp.int32, (tree, 1), 0)
    firsts = range(0, onehot_ref.shape[0], tree)
    parents = [parents_ref[first:first + tree, :] - first for first in firsts]
    jumps = [(parent == lanes).astype(BF16) for parent in parents]
    depths = [jnp.broadcast_to((parent != rows).astype(F32), (tree, 128)) for parent in parents]
    for level in range((tree - 1).bit_length()):
        depths = [
            depth + jnp.dot(jump, depth.astype(BF16), preferred_element_type=F32)
            for depth, jump in zip(depths, jumps)
        ]
        jumps = [jnp.dot(jump, jump, preferred_element_type=F32).astype(BF16) for jump in jumps]
    for first, depth in zip(firsts, depths):
        onehot_ref[first:first + tree, :] = (depth[:, :1].astype(jnp.int32) == lanes).astype(BF16)


def depth_onehot(parents, tree):
    rows = parents.shape[0]
    return pl.pallas_call(
        functools.partial(onehot_kernel, tree),
        name="onehot",
        out_shape=jax.ShapeDtypeStruct((rows, tree), BF16),
        compiler_params=params(16),
        cost_estimate=cost(48 * rows * tree * tree, 8 * rows * tree),
    )(parents[:, None])


def forward_kernel(place_ref, near_ref, far_ref, *refs):
    out_ref = refs[-1]
    outer = jnp.logical_or(place_ref[1] == 0, place_ref[1] == 3)

    @pl.when(outer)
    def _():
        out_ref[...] = near_ref[...]

    @pl.when(jnp.logical_not(outer))
    def _():
        out_ref[...] = far_ref[...]


def forward(place, near, far, after, long):
    return pl.pallas_call(
        forward_kernel,
        name="forward",
        out_shape=jax.ShapeDtypeStruct(near.shape, near.dtype),
        in_specs=[SMEM, VMEM, VMEM] + [ANY] * len(after),
        out_specs=VMEM,
        compiler_params=params(8),
        cost_estimate=cost(0, 6 * near.size, long),
    )(place, near, far, *after)


def slot_of(dest, chips, gx):
    ahead = lax.rem(dest // 2 - gx // 2 + 2 * chips - 1, chips)
    return jnp.where(lax.rem(gx, 2) == lax.rem(dest, 2), chips, 0) + ahead


def look_kernel(count, chips, block, first, exclusive, place_ref, onehot_ref, table_ref, *refs):
    looked_ref = refs[-1]
    size = looked_ref.shape[0] // count
    for dest in range(count):
        here = pl.ds(dest * block + first, size)
        looked = jnp.dot(onehot_ref[here, :], table_ref[...], preferred_element_type=F32)
        slot = pl.multiple_of(slot_of(dest, chips, place_ref[0]) * size, 16)
        looked_ref[pl.ds(slot, size), :] = looked.astype(BF16)


def look(chips, count, block, first, size, exclusive, place, onehot, table, after):
    depth = table.shape[1]
    tile = divisor(depth, (896, 512, 256, 128))
    return pl.pallas_call(
        functools.partial(look_kernel, count, chips, block, first, exclusive),
        name="look",
        grid=(depth // tile,),
        out_shape=jax.ShapeDtypeStruct((count * size, depth), BF16),
        in_specs=[SMEM, pl.BlockSpec(onehot.shape, lambda j: (0, 0)), pl.BlockSpec((table.shape[0], tile), lambda j: (0, j))]
        + [ANY] * len(after),
        out_specs=pl.BlockSpec((count * size, tile), lambda j: (0, j)),
        compiler_params=params(16),
        cost_estimate=cost(2 * count * size * table.shape[0] * depth, 4 * count * size * depth),
    )(place, onehot, table, *after)


def arrange_kernel(count, chips, exclusive, added, place_ref, *refs):
    rows_ref = refs[-1]
    size = rows_ref.shape[0] // count
    for held in range(count):
        dest = lax.bitwise_xor(place_ref[1], held) if exclusive else held
        here = pl.ds(pl.multiple_of(slot_of(dest, chips, place_ref[0]) * size, 16), size)
        if added:
            rows_ref[here, :] = (refs[held][...].astype(F32) + refs[count][here, :].astype(F32)).astype(BF16)
        else:
            rows_ref[here, :] = refs[held][...]


def arrange(chips, exclusive, place, held, looked, after):
    count = len(held)
    size, depth = held[0].shape
    added = [] if looked is None else [looked]
    return pl.pallas_call(
        functools.partial(arrange_kernel, count, chips, exclusive, bool(added)),
        name="arrange",
        out_shape=jax.ShapeDtypeStruct((count * size, depth), BF16),
        in_specs=[SMEM] + [VMEM] * (count + len(added)) + [ANY] * len(after),
        out_specs=VMEM,
        compiler_params=params(16),
        cost_estimate=cost(count * size * depth, 6 * count * size * depth),
    )(place, *held, *added, *after)


def embed_own_kernel(block, first, place_ref, onehot_ref, table_ref, hidden_ref, *refs):
    start = place_ref[1] * block
    for rows_ref in refs:
        size = rows_ref.shape[0]
        here = pl.ds(pl.multiple_of(start + first, 16), size)
        looked = jnp.dot(onehot_ref[here, :], table_ref[...], preferred_element_type=F32)
        rows_ref[...] = (hidden_ref[first:first + size, :].astype(F32) + looked).astype(BF16)
        first += size


def embed_own(sizes, place, onehot, table, hidden):
    block, depth = hidden.shape
    tile = divisor(depth, (896, 512, 256, 128))
    column = lambda j: (0, j)
    return pl.pallas_call(
        functools.partial(embed_own_kernel, block, block - sum(sizes)),
        name="own",
        grid=(depth // tile,),
        out_shape=[jax.ShapeDtypeStruct((size, depth), BF16) for size in sizes],
        in_specs=[
            SMEM,
            pl.BlockSpec(onehot.shape, lambda j: (0, 0)),
            pl.BlockSpec((table.shape[0], tile), column),
            pl.BlockSpec((block, tile), column),
        ],
        out_specs=[pl.BlockSpec((size, tile), column) for size in sizes],
        compiler_params=params(16),
        cost_estimate=cost(2 * sum(sizes) * table.shape[0] * depth, 6 * sum(sizes) * depth),
    )(place, onehot, table, hidden)


def gelu_sum(terms):
    total = terms[0].astype(F32)
    for term in terms[1:]:
        total = total + term.astype(F32)
    return jax.nn.gelu(total, approximate=True).astype(BF16)


def product_kernel(start, tile, steps, slots, ending, rows_ref, lead_ref, weight_ref, *refs):
    terms = refs[:ending[3]]
    outs = 2 if not ending[3] else 3
    scratch = len(refs) - (2 if not ending[3] else 6)
    send_ref, keep_ref = refs[scratch - outs:scratch - outs + 2]
    held, arrived = refs[scratch:scratch + 2]
    half = send_ref.shape[0]
    step = pl.program_id(0)

    def fetch(index):
        column = pl.multiple_of(start + index * tile, 128)
        slot = lax.rem(index, slots)
        return pltpu.make_async_copy(weight_ref.at[:, pl.ds(column, tile)], held.at[slot], arrived.at[slot])

    if ending[3]:
        out_ref = refs[scratch - 1]
        term_buffer, out_buffer, term_sems, out_sem = refs[scratch + 2:]
        row, column, width, number = ending
        given = [pltpu.make_async_copy(terms[n], term_buffer.at[n], term_sems.at[n]) for n in range(number)]
        place_out = out_ref.at[row:row + out_buffer.shape[0], column:column + width]
        taken = pltpu.make_async_copy(out_buffer, place_out, out_sem.at[0])

    @pl.when(step == 0)
    def _():
        for index in range(1, min(slots - 1, steps)):
            fetch(index).start()
        if ending[3]:
            for copy in given:
                copy.start()

    @pl.when(step + slots - 1 < steps)
    def _():
        fetch(step + slots - 1).start()

    def multiply(tile_ref):
        out = jnp.dot(rows_ref[...], tile_ref[...], preferred_element_type=F32)
        send_ref[...] = out[:half].astype(BF16)
        keep_ref[...] = out[half:].astype(BF16)

    @pl.when(step == 0)
    def _():
        multiply(lead_ref)

    @pl.when(step > 0)
    def _():
        fetch(step).wait()
        multiply(held.at[lax.rem(step, slots)])

    if ending[3]:
        @pl.when(step == 0)
        def _():
            for copy in given:
                copy.wait()
            part = divisor(width, (512, 384, 256, 128))

            @pl.loop(0, width // part)
            def _(index):
                here = pl.ds(pl.multiple_of(index * part, 128), part)
                out_buffer[:, here] = gelu_sum([term_buffer[n, :, here] for n in range(number)])

            taken.start()

        @pl.when(step == steps - 1)
        def _():
            taken.wait()


def tile_of(width):
    return divisor(width, (512, 384, 256, 128))


def product(rows, lead, weight, start, width, after, ending=None, terms=(), out=None, shape=None):
    height, depth = rows.shape
    tile = lead.shape[1]
    slots = 4
    half = jax.ShapeDtypeStruct((height // 2, width), BF16)
    outs = [half, half]
    out_specs = [pl.BlockSpec((height // 2, tile), lambda j: (0, j))] * 2
    scratch = [
        pltpu.VMEM((slots, depth, tile), BF16),
        pltpu.SemaphoreType.DMA((slots,)),
    ]
    operands = [rows, lead, weight, *terms]
    aliases = {}
    ending = (0, 0, 0, 0) if not terms else (*ending, terms[0].shape[1], len(terms))
    if terms:
        outs.append(jax.ShapeDtypeStruct(shape, BF16))
        out_specs.append(ANY)
        scratch += [
            pltpu.VMEM((len(terms), *terms[0].shape), BF16),
            pltpu.VMEM(terms[0].shape, BF16),
            pltpu.SemaphoreType.DMA((len(terms),)),
            pltpu.SemaphoreType.DMA((1,)),
        ]
        if out is not None:
            aliases = {len(operands): 2}
            operands.append(out)
    operands += after
    return pl.pallas_call(
        functools.partial(product_kernel, start, tile, width // tile, slots, ending),
        name="product",
        grid=(width // tile,),
        out_shape=outs,
        in_specs=[VMEM] * 2 + [ANY] * (len(operands) - 2),
        out_specs=out_specs,
        scratch_shapes=scratch,
        input_output_aliases=aliases,
        compiler_params=params(24),
        cost_estimate=cost(2 * height * depth * width, 2 * (height * depth + depth * width + height * width)),
    )(*operands)


def pair_kernel(keep_ref, got_ref, *refs):
    away_ref, stay_ref = refs[-2:]
    cut = away_ref.shape[0]
    total = keep_ref[...].astype(F32) + got_ref[...].astype(F32)
    away_ref[...] = total[:cut].astype(BF16)
    stay_ref[...] = total[cut:].astype(BF16)


def pair(chips, keep, got, after, long):
    height, width = keep.shape
    size = height // chips
    tile = width // 2 if width % 256 == 0 else width
    spec = lambda rows: pl.BlockSpec((rows, tile), lambda j: (0, j))
    return pl.pallas_call(
        pair_kernel,
        name="pair",
        grid=(width // tile,),
        out_shape=[jax.ShapeDtypeStruct((height - size, width), BF16), jax.ShapeDtypeStruct((size, width), BF16)],
        in_specs=[spec(height), spec(height)] + [ANY] * len(after),
        out_specs=[spec(height - size), spec(size)],
        compiler_params=params(16),
        cost_estimate=cost(height * width, 6 * height * width, long),
    )(keep, got, *after)


def finish_kernel(count, *refs):
    out_ref, token_ref = refs[-2:]
    out_ref[...] = gelu_sum([refs[index][...] for index in range(count)])
    token_ref[...] = jnp.zeros_like(token_ref)


def finish(shape, step, rows, terms, held, after, long):
    index, start, width = step
    tile = divisor(width, (1536, 1152, 768, 512, 384, 256, 128))
    aliases = {} if held is None else {len(terms): 0}
    return pl.pallas_call(
        functools.partial(finish_kernel, len(terms)),
        name="finish",
        grid=(width // tile,),
        out_shape=[jax.ShapeDtypeStruct(shape, BF16), jax.ShapeDtypeStruct((8, 128), F32)],
        in_specs=[pl.BlockSpec((rows, tile), lambda j: (0, j))] * len(terms) + [ANY] * (len(aliases) + len(after)),
        out_specs=[
            pl.BlockSpec((rows, tile), lambda j: (index, start // tile + j)),
            pl.BlockSpec((8, 128), lambda j: (0, 0)),
        ],
        input_output_aliases=aliases,
        compiler_params=params(16),
        cost_estimate=cost(12 * rows * width, 6 * rows * width, long),
    )(*terms, *([] if held is None else [held]), *after)


def column_pieces(columns, shares):
    unit, start, pieces = columns // sum(shares), 0, []
    for share in shares:
        pieces.append((start, share * unit))
        start += share * unit
    return pieces


SHARES = ((8, 10), (6, 6, 6), (6, 6, 6))


def chunk_sizes(block):
    if block % 192 == 0:
        return [block // 4, block * 5 // 12, block // 3]
    return [block // 3] * 3


ORDER = (
    ("f0", "a0", "p00", "p01", "s00", "f1", "s01"),
    ("a1", "t2", "p10", "p11-00", "f2", "s10", "p12-01", "s11"),
    ("a2", "p20-10", "s12", "p21-11", "s20", "p22-12+", "g20!"),
    ("s21!", "s22", "g21", "g22"),
)


def local(n_gx, n_gy, hidden, parents, depth_table, weight):
    tree = depth_table.shape[0]
    columns = weight.shape[1]
    block = hidden.shape[0]
    chips = n_gx // 2
    sizes = chunk_sizes(block)
    firsts = [sum(sizes[:index]) for index in range(len(sizes))]
    parts = len(sizes)
    place = jnp.stack([lax.axis_index("gx"), lax.axis_index("gy")]).astype(jnp.int32)

    exclusive = n_gy == 4

    def swap(array, distance):
        return lax.ppermute(array, "gy", [(k, k ^ distance) for k in range(n_gy)])

    def later(array, token):
        return lax.optimization_barrier((array, token))[0]

    def take(index, token):
        if not exclusive:
            whole = lax.all_gather(own[index], "gy", axis=0)
            held[index] = [whole[k] for k in range(n_gy)]
        else:
            rows = own[index] if token is None else later(own[index], token)
            held[index] = [own[index], None if index == 1 else swap(rows, 1), swap(rows, 2)]

    own, held = [hidden[:sizes[0]]], [None] * parts
    take(0, None)
    onehot = depth_onehot(parents, tree)
    own += embed_own(sizes[1:], place, onehot, depth_table, hidden)

    sibling = [(g, g ^ 1) for g in range(n_gx)]

    def across(ahead):
        return [(g, (g // 2 + ahead) % chips * 2 + g % 2) for g in range(n_gx)]

    pieces = [column_pieces(columns, shares) for shares in SHARES]
    cuts = sorted({(start, tile_of(width)) for each in pieces for start, width in each})
    leads = {(start, tile): weight[:, start:start + tile] for start, tile in cuts}

    out, after = None, own[1:2] + list(leads.values())
    products, sums, waiting = {}, {}, {}
    for item in sum(ORDER, ()):
        long = item.endswith("!")
        late = item.endswith("+")
        item = item.rstrip("!+")
        kind, index, piece = item[0], int(item[1]), item[1:3]
        if kind == "f":
            if exclusive:
                given = forward(place, held[index][1], held[index][2], after, long)
                held[index].append(lax.ppermute(given, "gy", [(0, 2), (1, 0), (2, 3), (3, 1)]))
                after = [given]
            if index == 0:
                take(1, after[0] if after else None)
                looked = look(chips, n_gx, block, 0, sizes[0], exclusive, place, onehot, depth_table, after)
        if kind == "t":
            take(index, after[0])
        if kind == "a":
            rows = arrange(chips, exclusive, place, held[index], None if index else looked, after)
            after = [rows]
            if exclusive and index == 0:
                held[1][1] = swap(later(own[1], rows), 1)
        if kind == "p":
            start, width = pieces[index][int(item[2])]
            extra = {}
            if len(item) > 3:
                done = item[4:]
                ending = (firsts[int(done[0])], pieces[int(done[0])][int(done[1])][0])
                extra = dict(ending=ending, terms=sums[done], out=out, shape=(block, columns))
            send, keep, *rest = product(rows, leads[start, tile_of(width)], weight, start, width, after, **extra)
            out = rest[0] if rest else out
            after = [keep]
            if late:
                waiting[piece] = keep, send
            else:
                products[piece] = keep, lax.ppermute(send, "gx", sibling)
        if kind == "s":
            away, stay = pair(chips, *products[piece], after, long)
            size = sizes[index]
            sums[piece] = [stay] + [
                lax.ppermute(away[(ahead - 1) * size:ahead * size], "gx", across(ahead)) for ahead in range(1, chips)
            ]
            after = [stay]
        if kind == "g":
            start, width = pieces[index][int(item[2])]
            out, token = finish((block, columns), (firsts[index] // sizes[index], start, width), sizes[index], sums[piece], out, after, long)
            after = [token]
            for name, (keep, send) in waiting.items():
                products[name] = keep, lax.ppermute(later(send, token), "gx", sibling)
            waiting = {}
    return out


def solution(mesh):
    return jax.shard_map(
        functools.partial(local, mesh.shape["gx"], mesh.shape["gy"]),
        mesh=mesh,
        in_specs=(P(("grp", "gy"), "gx"), P("grp"), P(None, "gx"), P("gx", "gy")),
        out_specs=P(("grp", "gx"), "gy"),
        check_vma=False,
    )
```

```python
import functools

import jax
import jax.numpy as jnp
from jax import lax
from jax.experimental import pallas as pl
from jax.experimental.pallas import tpu as pltpu
from jax.sharding import PartitionSpec as P

BF16 = jnp.bfloat16
F32 = jnp.float32
MIB = 1024 * 1024
ANY = pl.BlockSpec(memory_space=pl.ANY)
VMEM = pl.BlockSpec(memory_space=pltpu.VMEM)
SMEM = pl.BlockSpec(memory_space=pltpu.SMEM)


def params(limit):
    return pltpu.CompilerParams(vmem_limit_bytes=limit * MIB)


def cost(flops, accessed, long=False):
    factor = 1000 if long else 8
    return pl.CostEstimate(flops=factor * flops, bytes_accessed=factor * accessed, transcendentals=0)


def divisor(extent, choices):
    for choice in choices:
        if extent % choice == 0:
            return choice
    return extent


def onehot_kernel(tree, parents_ref, onehot_ref):
    lanes = lax.broadcasted_iota(jnp.int32, (tree, tree), 1)
    rows = lax.broadcasted_iota(jnp.int32, (tree, 1), 0)
    firsts = range(0, onehot_ref.shape[0], tree)
    parents = [parents_ref[first:first + tree, :] - first for first in firsts]
    jumps = [(parent == lanes).astype(BF16) for parent in parents]
    depths = [jnp.broadcast_to((parent != rows).astype(F32), (tree, 128)) for parent in parents]
    for level in range((tree - 1).bit_length()):
        depths = [
            depth + jnp.dot(jump, depth.astype(BF16), preferred_element_type=F32)
            for depth, jump in zip(depths, jumps)
        ]
        jumps = [jnp.dot(jump, jump, preferred_element_type=F32).astype(BF16) for jump in jumps]
    for first, depth in zip(firsts, depths):
        onehot_ref[first:first + tree, :] = (depth[:, :1].astype(jnp.int32) == lanes).astype(BF16)


def depth_onehot(parents, tree):
    rows = parents.shape[0]
    return pl.pallas_call(
        functools.partial(onehot_kernel, tree),
        name="onehot",
        out_shape=jax.ShapeDtypeStruct((rows, tree), BF16),
        compiler_params=params(16),
        cost_estimate=cost(48 * rows * tree * tree, 8 * rows * tree),
    )(parents[:, None])


def forward_kernel(place_ref, near_ref, far_ref, *refs):
    out_ref = refs[-1]
    outer = jnp.logical_or(place_ref[1] == 0, place_ref[1] == 3)

    @pl.when(outer)
    def _():
        out_ref[...] = near_ref[...]

    @pl.when(jnp.logical_not(outer))
    def _():
        out_ref[...] = far_ref[...]


def forward(place, near, far, after, long):
    return pl.pallas_call(
        forward_kernel,
        name="forward",
        out_shape=jax.ShapeDtypeStruct(near.shape, near.dtype),
        in_specs=[SMEM, VMEM, VMEM] + [ANY] * len(after),
        out_specs=VMEM,
        compiler_params=params(8),
        cost_estimate=cost(0, 6 * near.size, long),
    )(place, near, far, *after)


def slot_of(dest, chips, gx):
    ahead = lax.rem(dest // 2 - gx // 2 + 2 * chips - 1, chips)
    return jnp.where(lax.rem(gx, 2) == lax.rem(dest, 2), chips, 0) + ahead


def look_kernel(count, chips, block, first, exclusive, place_ref, onehot_ref, table_ref, *refs):
    looked_ref = refs[-1]
    size = looked_ref.shape[0] // count
    for dest in range(count):
        here = pl.ds(dest * block + first, size)
        looked = jnp.dot(onehot_ref[here, :], table_ref[...], preferred_element_type=F32)
        slot = pl.multiple_of(slot_of(dest, chips, place_ref[0]) * size, 16)
        looked_ref[pl.ds(slot, size), :] = looked.astype(BF16)


def look(chips, count, block, first, size, exclusive, place, onehot, table, after):
    depth = table.shape[1]
    tile = divisor(depth, (896, 512, 256, 128))
    return pl.pallas_call(
        functools.partial(look_kernel, count, chips, block, first, exclusive),
        name="look",
        grid=(depth // tile,),
        out_shape=jax.ShapeDtypeStruct((count * size, depth), BF16),
        in_specs=[SMEM, pl.BlockSpec(onehot.shape, lambda j: (0, 0)), pl.BlockSpec((table.shape[0], tile), lambda j: (0, j))]
        + [ANY] * len(after),
        out_specs=pl.BlockSpec((count * size, tile), lambda j: (0, j)),
        compiler_params=params(16),
        cost_estimate=cost(2 * count * size * table.shape[0] * depth, 4 * count * size * depth),
    )(place, onehot, table, *after)


def arrange_kernel(count, chips, exclusive, added, place_ref, *refs):
    rows_ref = refs[-1]
    size = rows_ref.shape[0] // count
    for held in range(count):
        dest = lax.bitwise_xor(place_ref[1], held) if exclusive else held
        here = pl.ds(pl.multiple_of(slot_of(dest, chips, place_ref[0]) * size, 16), size)
        if added:
            rows_ref[here, :] = (refs[held][...].astype(F32) + refs[count][here, :].astype(F32)).astype(BF16)
        else:
            rows_ref[here, :] = refs[held][...]


def arrange(chips, exclusive, place, held, looked, after):
    count = len(held)
    size, depth = held[0].shape
    added = [] if looked is None else [looked]
    return pl.pallas_call(
        functools.partial(arrange_kernel, count, chips, exclusive, bool(added)),
        name="arrange",
        out_shape=jax.ShapeDtypeStruct((count * size, depth), BF16),
        in_specs=[SMEM] + [VMEM] * (count + len(added)) + [ANY] * len(after),
        out_specs=VMEM,
        compiler_params=params(16),
        cost_estimate=cost(count * size * depth, 6 * count * size * depth),
    )(place, *held, *added, *after)


def embed_own_kernel(block, first, place_ref, onehot_ref, table_ref, hidden_ref, *refs):
    start = place_ref[1] * block
    for rows_ref in refs:
        size = rows_ref.shape[0]
        here = pl.ds(pl.multiple_of(start + first, 16), size)
        looked = jnp.dot(onehot_ref[here, :], table_ref[...], preferred_element_type=F32)
        rows_ref[...] = (hidden_ref[first:first + size, :].astype(F32) + looked).astype(BF16)
        first += size


def embed_own(sizes, place, onehot, table, hidden):
    block, depth = hidden.shape
    tile = divisor(depth, (896, 512, 256, 128))
    column = lambda j: (0, j)
    return pl.pallas_call(
        functools.partial(embed_own_kernel, block, block - sum(sizes)),
        name="own",
        grid=(depth // tile,),
        out_shape=[jax.ShapeDtypeStruct((size, depth), BF16) for size in sizes],
        in_specs=[
            SMEM,
            pl.BlockSpec(onehot.shape, lambda j: (0, 0)),
            pl.BlockSpec((table.shape[0], tile), column),
            pl.BlockSpec((block, tile), column),
        ],
        out_specs=[pl.BlockSpec((size, tile), column) for size in sizes],
        compiler_params=params(16),
        cost_estimate=cost(2 * sum(sizes) * table.shape[0] * depth, 6 * sum(sizes) * depth),
    )(place, onehot, table, hidden)


def gelu_sum(terms):
    total = terms[0].astype(F32)
    for term in terms[1:]:
        total = total + term.astype(F32)
    return jax.nn.gelu(total, approximate=True).astype(BF16)


def product_kernel(start, tile, steps, slots, ending, rows_ref, lead_ref, weight_ref, *refs):
    terms = refs[:ending[3]]
    outs = 2 if not ending[3] else 3
    scratch = len(refs) - (2 if not ending[3] else 6)
    send_ref, keep_ref = refs[scratch - outs:scratch - outs + 2]
    held, arrived = refs[scratch:scratch + 2]
    half = send_ref.shape[0]
    step = pl.program_id(0)

    def fetch(index):
        column = pl.multiple_of(start + index * tile, 128)
        slot = lax.rem(index, slots)
        return pltpu.make_async_copy(weight_ref.at[:, pl.ds(column, tile)], held.at[slot], arrived.at[slot])

    if ending[3]:
        out_ref = refs[scratch - 1]
        term_buffer, out_buffer, term_sems, out_sem = refs[scratch + 2:]
        row, column, width, number = ending
        given = [pltpu.make_async_copy(terms[n], term_buffer.at[n], term_sems.at[n]) for n in range(number)]
        place_out = out_ref.at[row:row + out_buffer.shape[0], column:column + width]
        taken = pltpu.make_async_copy(out_buffer, place_out, out_sem.at[0])

    @pl.when(step == 0)
    def _():
        for index in range(1, min(slots - 1, steps)):
            fetch(index).start()
        if ending[3]:
            for copy in given:
                copy.start()

    @pl.when(step + slots - 1 < steps)
    def _():
        fetch(step + slots - 1).start()

    def multiply(tile_ref):
        out = jnp.dot(rows_ref[...], tile_ref[...], preferred_element_type=F32)
        send_ref[...] = out[:half].astype(BF16)
        keep_ref[...] = out[half:].astype(BF16)

    @pl.when(step == 0)
    def _():
        multiply(lead_ref)

    @pl.when(step > 0)
    def _():
        fetch(step).wait()
        multiply(held.at[lax.rem(step, slots)])

    if ending[3]:
        @pl.when(step == 0)
        def _():
            for copy in given:
                copy.wait()
            part = divisor(width, (512, 384, 256, 128))

            @pl.loop(0, width // part)
            def _(index):
                here = pl.ds(pl.multiple_of(index * part, 128), part)
                out_buffer[:, here] = gelu_sum([term_buffer[n, :, here] for n in range(number)])

            taken.start()

        @pl.when(step == steps - 1)
        def _():
            taken.wait()


def tile_of(width):
    return divisor(width, (512, 384, 256, 128))


def product(rows, lead, weight, start, width, after, ending=None, terms=(), out=None, shape=None):
    height, depth = rows.shape
    tile = lead.shape[1]
    slots = 4
    half = jax.ShapeDtypeStruct((height // 2, width), BF16)
    outs = [half, half]
    out_specs = [pl.BlockSpec((height // 2, tile), lambda j: (0, j))] * 2
    scratch = [
        pltpu.VMEM((slots, depth, tile), BF16),
        pltpu.SemaphoreType.DMA((slots,)),
    ]
    operands = [rows, lead, weight, *terms]
    aliases = {}
    ending = (0, 0, 0, 0) if not terms else (*ending, terms[0].shape[1], len(terms))
    if terms:
        outs.append(jax.ShapeDtypeStruct(shape, BF16))
        out_specs.append(ANY)
        scratch += [
            pltpu.VMEM((len(terms), *terms[0].shape), BF16),
            pltpu.VMEM(terms[0].shape, BF16),
            pltpu.SemaphoreType.DMA((len(terms),)),
            pltpu.SemaphoreType.DMA((1,)),
        ]
        if out is not None:
            aliases = {len(operands): 2}
            operands.append(out)
    operands += after
    return pl.pallas_call(
        functools.partial(product_kernel, start, tile, width // tile, slots, ending),
        name="product",
        grid=(width // tile,),
        out_shape=outs,
        in_specs=[VMEM] * 2 + [ANY] * (len(operands) - 2),
        out_specs=out_specs,
        scratch_shapes=scratch,
        input_output_aliases=aliases,
        compiler_params=params(24),
        cost_estimate=cost(2 * height * depth * width, 2 * (height * depth + depth * width + height * width)),
    )(*operands)


def pair_kernel(keep_ref, got_ref, *refs):
    away_ref, stay_ref = refs[-2:]
    cut = away_ref.shape[0]
    total = keep_ref[...].astype(F32) + got_ref[...].astype(F32)
    away_ref[...] = total[:cut].astype(BF16)
    stay_ref[...] = total[cut:].astype(BF16)


def pair(chips, keep, got, after, long):
    height, width = keep.shape
    size = height // chips
    tile = width // 2 if width % 256 == 0 else width
    spec = lambda rows: pl.BlockSpec((rows, tile), lambda j: (0, j))
    return pl.pallas_call(
        pair_kernel,
        name="pair",
        grid=(width // tile,),
        out_shape=[jax.ShapeDtypeStruct((height - size, width), BF16), jax.ShapeDtypeStruct((size, width), BF16)],
        in_specs=[spec(height), spec(height)] + [ANY] * len(after),
        out_specs=[spec(height - size), spec(size)],
        compiler_params=params(16),
        cost_estimate=cost(height * width, 6 * height * width, long),
    )(keep, got, *after)


def finish_kernel(count, *refs):
    out_ref, token_ref = refs[-2:]
    out_ref[...] = gelu_sum([refs[index][...] for index in range(count)])
    token_ref[...] = jnp.zeros_like(token_ref)


def finish(shape, step, rows, terms, held, after, long):
    index, start, width = step
    tile = divisor(width, (1536, 1152, 768, 512, 384, 256, 128))
    aliases = {} if held is None else {len(terms): 0}
    return pl.pallas_call(
        functools.partial(finish_kernel, len(terms)),
        name="finish",
        grid=(width // tile,),
        out_shape=[jax.ShapeDtypeStruct(shape, BF16), jax.ShapeDtypeStruct((8, 128), F32)],
        in_specs=[pl.BlockSpec((rows, tile), lambda j: (0, j))] * len(terms) + [ANY] * (len(aliases) + len(after)),
        out_specs=[
            pl.BlockSpec((rows, tile), lambda j: (index, start // tile + j)),
            pl.BlockSpec((8, 128), lambda j: (0, 0)),
        ],
        input_output_aliases=aliases,
        compiler_params=params(16),
        cost_estimate=cost(12 * rows * width, 6 * rows * width, long),
    )(*terms, *([] if held is None else [held]), *after)


def column_pieces(columns, shares):
    unit, start, pieces = columns // sum(shares), 0, []
    for share in shares:
        pieces.append((start, share * unit))
        start += share * unit
    return pieces


SHARES = ((9, 9), (6, 6, 6), (6, 6, 6))


def chunk_sizes(block):
    if block % 192 == 0:
        return [block // 4, block * 5 // 12, block // 3]
    return [block // 3] * 3


ORDER = (
    ("f0", "a0", "p00", "p01", "s00", "f1", "s01"),
    ("a1", "t2", "p10", "p11-00", "f2", "s10", "p12-01", "s11"),
    ("a2", "p20-10", "s12", "p21-11", "s20", "p22-12+", "g20!"),
    ("s21!", "s22", "g21", "g22"),
)


def local(n_gx, n_gy, hidden, parents, depth_table, weight):
    tree = depth_table.shape[0]
    columns = weight.shape[1]
    block = hidden.shape[0]
    chips = n_gx // 2
    sizes = chunk_sizes(block)
    firsts = [sum(sizes[:index]) for index in range(len(sizes))]
    parts = len(sizes)
    place = jnp.stack([lax.axis_index("gx"), lax.axis_index("gy")]).astype(jnp.int32)

    exclusive = n_gy == 4

    def swap(array, distance):
        return lax.ppermute(array, "gy", [(k, k ^ distance) for k in range(n_gy)])

    def later(array, token):
        return lax.optimization_barrier((array, token))[0]

    def take(index, token):
        if not exclusive:
            whole = lax.all_gather(own[index], "gy", axis=0)
            held[index] = [whole[k] for k in range(n_gy)]
        else:
            rows = own[index] if token is None else later(own[index], token)
            held[index] = [own[index], None if index == 1 else swap(rows, 1), swap(rows, 2)]

    own, held = [hidden[:sizes[0]]], [None] * parts
    take(0, None)
    onehot = depth_onehot(parents, tree)
    own += embed_own(sizes[1:], place, onehot, depth_table, hidden)

    sibling = [(g, g ^ 1) for g in range(n_gx)]

    def across(ahead):
        return [(g, (g // 2 + ahead) % chips * 2 + g % 2) for g in range(n_gx)]

    out, after = None, own[1:2]
    pieces = [column_pieces(columns, shares) for shares in SHARES]
    products, sums, waiting = {}, {}, {}
    for item in sum(ORDER, ()):
        long = item.endswith("!")
        late = item.endswith("+")
        item = item.rstrip("!+")
        kind, index, piece = item[0], int(item[1]), item[1:3]
        if kind == "f":
            if exclusive:
                given = forward(place, held[index][1], held[index][2], after, long)
                held[index].append(lax.ppermute(given, "gy", [(0, 2), (1, 0), (2, 3), (3, 1)]))
                after = [given]
            if index == 0:
                take(1, after[0] if after else None)
                looked = look(chips, n_gx, block, 0, sizes[0], exclusive, place, onehot, depth_table, after)
                cuts = sorted({(start, tile_of(width)) for each in pieces for start, width in each})
                ready = later(weight, looked)
                leads = {(start, tile): ready[:, start:start + tile] for start, tile in cuts}
        if kind == "t":
            take(index, after[0])
        if kind == "a":
            rows = arrange(chips, exclusive, place, held[index], None if index else looked, after)
            after = [rows]
            if exclusive and index == 0:
                held[1][1] = swap(later(own[1], rows), 1)
        if kind == "p":
            start, width = pieces[index][int(item[2])]
            extra = {}
            if len(item) > 3:
                done = item[4:]
                ending = (firsts[int(done[0])], pieces[int(done[0])][int(done[1])][0])
                extra = dict(ending=ending, terms=sums[done], out=out, shape=(block, columns))
            send, keep, *rest = product(rows, leads[start, tile_of(width)], weight, start, width, after, **extra)
            out = rest[0] if rest else out
            after = [keep]
            if late:
                waiting[piece] = keep, send
            else:
                products[piece] = keep, lax.ppermute(send, "gx", sibling)
        if kind == "s":
            away, stay = pair(chips, *products[piece], after, long)
            size = sizes[index]
            sums[piece] = [stay] + [
                lax.ppermute(away[(ahead - 1) * size:ahead * size], "gx", across(ahead)) for ahead in range(1, chips)
            ]
            after = [stay]
        if kind == "g":
            start, width = pieces[index][int(item[2])]
            out, token = finish((block, columns), (firsts[index] // sizes[index], start, width), sizes[index], sums[piece], out, after, long)
            after = [token]
            for name, (keep, send) in waiting.items():
                products[name] = keep, lax.ppermute(later(send, token), "gx", sibling)
            waiting = {}
    return out


def solution(mesh):
    return jax.shard_map(
        functools.partial(local, mesh.shape["gx"], mesh.shape["gy"]),
        mesh=mesh,
        in_specs=(P(("grp", "gy"), "gx"), P("grp"), P(None, "gx"), P("gx", "gy")),
        out_specs=P(("grp", "gx"), "gy"),
        check_vma=False,
    )
```

```python
import functools

import jax
import jax.numpy as jnp
from jax import lax
from jax.experimental import pallas as pl
from jax.experimental.pallas import tpu as pltpu
from jax.sharding import PartitionSpec as P

BF16 = jnp.bfloat16
F32 = jnp.float32
MIB = 1024 * 1024
ANY = pl.BlockSpec(memory_space=pl.ANY)
VMEM = pl.BlockSpec(memory_space=pltpu.VMEM)
SMEM = pl.BlockSpec(memory_space=pltpu.SMEM)


def params(limit):
    return pltpu.CompilerParams(vmem_limit_bytes=limit * MIB)


def cost(flops, accessed, long=False):
    factor = 1000 if long else 8
    return pl.CostEstimate(flops=factor * flops, bytes_accessed=factor * accessed, transcendentals=0)


def divisor(extent, choices):
    for choice in choices:
        if extent % choice == 0:
            return choice
    return extent


def onehot_kernel(tree, parents_ref, onehot_ref):
    lanes = lax.broadcasted_iota(jnp.int32, (tree, tree), 1)
    rows = lax.broadcasted_iota(jnp.int32, (tree, 1), 0)
    firsts = range(0, onehot_ref.shape[0], tree)
    parents = [parents_ref[first:first + tree, :] - first for first in firsts]
    jumps = [(parent == lanes).astype(BF16) for parent in parents]
    depths = [jnp.broadcast_to((parent != rows).astype(F32), (tree, 128)) for parent in parents]
    for level in range((tree - 1).bit_length()):
        depths = [
            depth + jnp.dot(jump, depth.astype(BF16), preferred_element_type=F32)
            for depth, jump in zip(depths, jumps)
        ]
        jumps = [jnp.dot(jump, jump, preferred_element_type=F32).astype(BF16) for jump in jumps]
    for first, depth in zip(firsts, depths):
        onehot_ref[first:first + tree, :] = (depth[:, :1].astype(jnp.int32) == lanes).astype(BF16)


def depth_onehot(parents, tree):
    rows = parents.shape[0]
    return pl.pallas_call(
        functools.partial(onehot_kernel, tree),
        name="onehot",
        out_shape=jax.ShapeDtypeStruct((rows, tree), BF16),
        compiler_params=params(16),
        cost_estimate=cost(48 * rows * tree * tree, 8 * rows * tree),
    )(parents[:, None])


def forward_kernel(place_ref, near_ref, far_ref, *refs):
    out_ref = refs[-1]
    outer = jnp.logical_or(place_ref[1] == 0, place_ref[1] == 3)

    @pl.when(outer)
    def _():
        out_ref[...] = near_ref[...]

    @pl.when(jnp.logical_not(outer))
    def _():
        out_ref[...] = far_ref[...]


def forward(place, near, far, after, long):
    return pl.pallas_call(
        forward_kernel,
        name="forward",
        out_shape=jax.ShapeDtypeStruct(near.shape, near.dtype),
        in_specs=[SMEM, VMEM, VMEM] + [ANY] * len(after),
        out_specs=VMEM,
        compiler_params=params(8),
        cost_estimate=cost(0, 6 * near.size, long),
    )(place, near, far, *after)


def slot_of(dest, chips, gx):
    ahead = lax.rem(dest // 2 - gx // 2 + 2 * chips - 1, chips)
    return jnp.where(lax.rem(gx, 2) == lax.rem(dest, 2), chips, 0) + ahead


def look_kernel(count, chips, block, first, exclusive, place_ref, onehot_ref, table_ref, *refs):
    looked_ref = refs[-1]
    size = looked_ref.shape[0] // count
    for dest in range(count):
        here = pl.ds(dest * block + first, size)
        looked = jnp.dot(onehot_ref[here, :], table_ref[...], preferred_element_type=F32)
        slot = pl.multiple_of(slot_of(dest, chips, place_ref[0]) * size, 16)
        looked_ref[pl.ds(slot, size), :] = looked.astype(BF16)


def look(chips, count, block, first, size, exclusive, place, onehot, table, after):
    depth = table.shape[1]
    tile = divisor(depth, (896, 512, 256, 128))
    return pl.pallas_call(
        functools.partial(look_kernel, count, chips, block, first, exclusive),
        name="look",
        grid=(depth // tile,),
        out_shape=jax.ShapeDtypeStruct((count * size, depth), BF16),
        in_specs=[SMEM, pl.BlockSpec(onehot.shape, lambda j: (0, 0)), pl.BlockSpec((table.shape[0], tile), lambda j: (0, j))]
        + [ANY] * len(after),
        out_specs=pl.BlockSpec((count * size, tile), lambda j: (0, j)),
        compiler_params=params(16),
        cost_estimate=cost(2 * count * size * table.shape[0] * depth, 4 * count * size * depth),
    )(place, onehot, table, *after)


def arrange_kernel(count, chips, exclusive, added, place_ref, *refs):
    rows_ref = refs[-1]
    size = rows_ref.shape[0] // count
    for held in range(count):
        dest = lax.bitwise_xor(place_ref[1], held) if exclusive else held
        here = pl.ds(pl.multiple_of(slot_of(dest, chips, place_ref[0]) * size, 16), size)
        if added:
            rows_ref[here, :] = (refs[held][...].astype(F32) + refs[count][here, :].astype(F32)).astype(BF16)
        else:
            rows_ref[here, :] = refs[held][...]


def arrange(chips, exclusive, place, held, looked, after):
    count = len(held)
    size, depth = held[0].shape
    added = [] if looked is None else [looked]
    return pl.pallas_call(
        functools.partial(arrange_kernel, count, chips, exclusive, bool(added)),
        name="arrange",
        out_shape=jax.ShapeDtypeStruct((count * size, depth), BF16),
        in_specs=[SMEM] + [VMEM] * (count + len(added)) + [ANY] * len(after),
        out_specs=VMEM,
        compiler_params=params(16),
        cost_estimate=cost(count * size * depth, 6 * count * size * depth),
    )(place, *held, *added, *after)


def embed_own_kernel(block, first, place_ref, onehot_ref, table_ref, hidden_ref, *refs):
    start = place_ref[1] * block
    for rows_ref in refs:
        size = rows_ref.shape[0]
        here = pl.ds(pl.multiple_of(start + first, 16), size)
        looked = jnp.dot(onehot_ref[here, :], table_ref[...], preferred_element_type=F32)
        rows_ref[...] = (hidden_ref[first:first + size, :].astype(F32) + looked).astype(BF16)
        first += size


def embed_own(sizes, place, onehot, table, hidden):
    block, depth = hidden.shape
    tile = divisor(depth, (896, 512, 256, 128))
    column = lambda j: (0, j)
    return pl.pallas_call(
        functools.partial(embed_own_kernel, block, block - sum(sizes)),
        name="own",
        grid=(depth // tile,),
        out_shape=[jax.ShapeDtypeStruct((size, depth), BF16) for size in sizes],
        in_specs=[
            SMEM,
            pl.BlockSpec(onehot.shape, lambda j: (0, 0)),
            pl.BlockSpec((table.shape[0], tile), column),
            pl.BlockSpec((block, tile), column),
        ],
        out_specs=[pl.BlockSpec((size, tile), column) for size in sizes],
        compiler_params=params(16),
        cost_estimate=cost(2 * sum(sizes) * table.shape[0] * depth, 6 * sum(sizes) * depth),
    )(place, onehot, table, hidden)


def gelu_sum(terms):
    total = terms[0].astype(F32)
    for term in terms[1:]:
        total = total + term.astype(F32)
    return jax.nn.gelu(total, approximate=True).astype(BF16)


def product_kernel(start, tile, steps, slots, ending, rows_ref, lead_ref, weight_ref, *refs):
    terms = refs[:ending[3]]
    outs = 2 if not ending[3] else 3
    scratch = len(refs) - (2 if not ending[3] else 6)
    send_ref, keep_ref = refs[scratch - outs:scratch - outs + 2]
    held, arrived = refs[scratch:scratch + 2]
    half = send_ref.shape[0]
    step = pl.program_id(0)

    def fetch(index):
        column = pl.multiple_of(start + index * tile, 128)
        slot = lax.rem(index, slots)
        return pltpu.make_async_copy(weight_ref.at[:, pl.ds(column, tile)], held.at[slot], arrived.at[slot])

    if ending[3]:
        out_ref = refs[scratch - 1]
        term_buffer, out_buffer, term_sems, out_sem = refs[scratch + 2:]
        row, column, width, number = ending
        given = [pltpu.make_async_copy(terms[n], term_buffer.at[n], term_sems.at[n]) for n in range(number)]
        place_out = out_ref.at[row:row + out_buffer.shape[0], column:column + width]
        taken = pltpu.make_async_copy(out_buffer, place_out, out_sem.at[0])

    @pl.when(step == 0)
    def _():
        for index in range(1, min(slots - 1, steps)):
            fetch(index).start()
        if ending[3]:
            for copy in given:
                copy.start()

    @pl.when(step + slots - 1 < steps)
    def _():
        fetch(step + slots - 1).start()

    def multiply(tile_ref):
        out = jnp.dot(rows_ref[...], tile_ref[...], preferred_element_type=F32)
        send_ref[...] = out[:half].astype(BF16)
        keep_ref[...] = out[half:].astype(BF16)

    @pl.when(step == 0)
    def _():
        multiply(lead_ref)

    @pl.when(step > 0)
    def _():
        fetch(step).wait()
        multiply(held.at[lax.rem(step, slots)])

    if ending[3]:
        @pl.when(step == 0)
        def _():
            for copy in given:
                copy.wait()
            part = divisor(width, (512, 384, 256, 128))

            @pl.loop(0, width // part)
            def _(index):
                here = pl.ds(pl.multiple_of(index * part, 128), part)
                out_buffer[:, here] = gelu_sum([term_buffer[n, :, here] for n in range(number)])

            taken.start()

        @pl.when(step == steps - 1)
        def _():
            taken.wait()


def tile_of(width):
    return divisor(width, (512, 384, 256, 128))


def product(rows, lead, weight, start, width, after, ending=None, terms=(), out=None, shape=None):
    height, depth = rows.shape
    tile = lead.shape[1]
    slots = 4
    half = jax.ShapeDtypeStruct((height // 2, width), BF16)
    outs = [half, half]
    out_specs = [pl.BlockSpec((height // 2, tile), lambda j: (0, j))] * 2
    scratch = [
        pltpu.VMEM((slots, depth, tile), BF16),
        pltpu.SemaphoreType.DMA((slots,)),
    ]
    operands = [rows, lead, weight, *terms]
    aliases = {}
    ending = (0, 0, 0, 0) if not terms else (*ending, terms[0].shape[1], len(terms))
    if terms:
        outs.append(jax.ShapeDtypeStruct(shape, BF16))
        out_specs.append(ANY)
        scratch += [
            pltpu.VMEM((len(terms), *terms[0].shape), BF16),
            pltpu.VMEM(terms[0].shape, BF16),
            pltpu.SemaphoreType.DMA((len(terms),)),
            pltpu.SemaphoreType.DMA((1,)),
        ]
        if out is not None:
            aliases = {len(operands): 2}
            operands.append(out)
    operands += after
    return pl.pallas_call(
        functools.partial(product_kernel, start, tile, width // tile, slots, ending),
        name="product",
        grid=(width // tile,),
        out_shape=outs,
        in_specs=[VMEM] * 2 + [ANY] * (len(operands) - 2),
        out_specs=out_specs,
        scratch_shapes=scratch,
        input_output_aliases=aliases,
        compiler_params=params(24),
        cost_estimate=cost(2 * height * depth * width, 2 * (height * depth + depth * width + height * width)),
    )(*operands)


def pair_kernel(keep_ref, got_ref, *refs):
    away_ref, stay_ref = refs[-2:]
    cut = away_ref.shape[0]
    total = keep_ref[...].astype(F32) + got_ref[...].astype(F32)
    away_ref[...] = total[:cut].astype(BF16)
    stay_ref[...] = total[cut:].astype(BF16)


def pair(chips, keep, got, after, long):
    height, width = keep.shape
    size = height // chips
    tile = width // 2 if width % 256 == 0 else width
    spec = lambda rows: pl.BlockSpec((rows, tile), lambda j: (0, j))
    return pl.pallas_call(
        pair_kernel,
        name="pair",
        grid=(width // tile,),
        out_shape=[jax.ShapeDtypeStruct((height - size, width), BF16), jax.ShapeDtypeStruct((size, width), BF16)],
        in_specs=[spec(height), spec(height)] + [ANY] * len(after),
        out_specs=[spec(height - size), spec(size)],
        compiler_params=params(16),
        cost_estimate=cost(height * width, 6 * height * width, long),
    )(keep, got, *after)


def finish_kernel(count, *refs):
    out_ref, token_ref = refs[-2:]
    out_ref[...] = gelu_sum([refs[index][...] for index in range(count)])
    token_ref[...] = jnp.zeros_like(token_ref)


def finish(shape, step, rows, terms, held, after, long):
    index, start, width = step
    tile = divisor(width, (1536, 1152, 768, 512, 384, 256, 128))
    aliases = {} if held is None else {len(terms): 0}
    return pl.pallas_call(
        functools.partial(finish_kernel, len(terms)),
        name="finish",
        grid=(width // tile,),
        out_shape=[jax.ShapeDtypeStruct(shape, BF16), jax.ShapeDtypeStruct((8, 128), F32)],
        in_specs=[pl.BlockSpec((rows, tile), lambda j: (0, j))] * len(terms) + [ANY] * (len(aliases) + len(after)),
        out_specs=[
            pl.BlockSpec((rows, tile), lambda j: (index, start // tile + j)),
            pl.BlockSpec((8, 128), lambda j: (0, 0)),
        ],
        input_output_aliases=aliases,
        compiler_params=params(16),
        cost_estimate=cost(12 * rows * width, 6 * rows * width, long),
    )(*terms, *([] if held is None else [held]), *after)


def column_pieces(columns, shares):
    unit, start, pieces = columns // sum(shares), 0, []
    for share in shares:
        pieces.append((start, share * unit))
        start += share * unit
    return pieces


SHARES = ((12, 6), (6, 6, 6), (6, 6, 6))


def chunk_sizes(block):
    if block % 192 == 0:
        return [block // 4, block * 5 // 12, block // 3]
    return [block // 3] * 3


ORDER = (
    ("f0", "a0", "p00", "f1", "p01", "s00"),
    ("a1", "t2", "p10", "s01", "p11-00", "f2", "s10", "p12-01", "s11"),
    ("a2", "p20-10", "s12", "p21-11", "s20", "p22-12+", "g20!"),
    ("s21!", "s22", "g21", "g22"),
)


def local(n_gx, n_gy, hidden, parents, depth_table, weight):
    tree = depth_table.shape[0]
    columns = weight.shape[1]
    block = hidden.shape[0]
    chips = n_gx // 2
    sizes = chunk_sizes(block)
    firsts = [sum(sizes[:index]) for index in range(len(sizes))]
    parts = len(sizes)
    place = jnp.stack([lax.axis_index("gx"), lax.axis_index("gy")]).astype(jnp.int32)

    exclusive = n_gy == 4

    def swap(array, distance):
        return lax.ppermute(array, "gy", [(k, k ^ distance) for k in range(n_gy)])

    def later(array, token):
        return lax.optimization_barrier((array, token))[0]

    def take(index, token):
        if not exclusive:
            whole = lax.all_gather(own[index], "gy", axis=0)
            held[index] = [whole[k] for k in range(n_gy)]
        else:
            rows = own[index] if token is None else later(own[index], token)
            held[index] = [own[index], None if index == 1 else swap(rows, 1), swap(rows, 2)]

    own, held = [hidden[:sizes[0]]], [None] * parts
    take(0, None)
    onehot = depth_onehot(parents, tree)
    own += embed_own(sizes[1:], place, onehot, depth_table, hidden)

    sibling = [(g, g ^ 1) for g in range(n_gx)]

    def across(ahead):
        return [(g, (g // 2 + ahead) % chips * 2 + g % 2) for g in range(n_gx)]

    out, after = None, own[1:2]
    pieces = [column_pieces(columns, shares) for shares in SHARES]
    products, sums, waiting = {}, {}, {}
    for item in sum(ORDER, ()):
        long = item.endswith("!")
        late = item.endswith("+")
        item = item.rstrip("!+")
        kind, index, piece = item[0], int(item[1]), item[1:3]
        if kind == "f":
            if exclusive:
                given = forward(place, held[index][1], held[index][2], after, long)
                held[index].append(lax.ppermute(given, "gy", [(0, 2), (1, 0), (2, 3), (3, 1)]))
                after = [given]
            if index == 0:
                take(1, after[0] if after else None)
                looked = look(chips, n_gx, block, 0, sizes[0], exclusive, place, onehot, depth_table, after)
                cuts = sorted({(start, tile_of(width)) for each in pieces for start, width in each})
                ready = later(weight, looked)
                if exclusive:
                    held[1][1] = swap(later(own[1], looked), 1)
                leads = {(start, tile): ready[:, start:start + tile] for start, tile in cuts}
        if kind == "t":
            take(index, after[0])
        if kind == "a":
            rows = arrange(chips, exclusive, place, held[index], None if index else looked, after)
            after = [rows]
        if kind == "p":
            start, width = pieces[index][int(item[2])]
            extra = {}
            if len(item) > 3:
                done = item[4:]
                ending = (firsts[int(done[0])], pieces[int(done[0])][int(done[1])][0])
                extra = dict(ending=ending, terms=sums[done], out=out, shape=(block, columns))
            send, keep, *rest = product(rows, leads[start, tile_of(width)], weight, start, width, after, **extra)
            out = rest[0] if rest else out
            after = [keep]
            if late:
                waiting[piece] = keep, send
            else:
                products[piece] = keep, lax.ppermute(send, "gx", sibling)
        if kind == "s":
            away, stay = pair(chips, *products[piece], after, long)
            size = sizes[index]
            sums[piece] = [stay] + [
                lax.ppermute(away[(ahead - 1) * size:ahead * size], "gx", across(ahead)) for ahead in range(1, chips)
            ]
            after = [stay]
        if kind == "g":
            start, width = pieces[index][int(item[2])]
            out, token = finish((block, columns), (firsts[index] // sizes[index], start, width), sizes[index], sums[piece], out, after, long)
            after = [token]
            for name, (keep, send) in waiting.items():
                products[name] = keep, lax.ppermute(later(send, token), "gx", sibling)
            waiting = {}
    return out


def solution(mesh):
    return jax.shard_map(
        functools.partial(local, mesh.shape["gx"], mesh.shape["gy"]),
        mesh=mesh,
        in_specs=(P(("grp", "gy"), "gx"), P("grp"), P(None, "gx"), P("gx", "gy")),
        out_specs=P(("grp", "gx"), "gy"),
        check_vma=False,
    )
```

```python
import functools

import jax
import jax.numpy as jnp
from jax import lax
from jax.experimental import pallas as pl
from jax.experimental.pallas import tpu as pltpu
from jax.sharding import PartitionSpec as P

BF16 = jnp.bfloat16
F32 = jnp.float32
MIB = 1024 * 1024
ANY = pl.BlockSpec(memory_space=pl.ANY)
VMEM = pl.BlockSpec(memory_space=pltpu.VMEM)
SMEM = pl.BlockSpec(memory_space=pltpu.SMEM)


def params(limit):
    return pltpu.CompilerParams(vmem_limit_bytes=limit * MIB)


def cost(flops, accessed, long=False):
    factor = 1000 if long else 8
    return pl.CostEstimate(flops=factor * flops, bytes_accessed=factor * accessed, transcendentals=0)


def divisor(extent, choices):
    for choice in choices:
        if extent % choice == 0:
            return choice
    return extent


def onehot_kernel(tree, parents_ref, onehot_ref):
    lanes = lax.broadcasted_iota(jnp.int32, (tree, tree), 1)
    rows = lax.broadcasted_iota(jnp.int32, (tree, 1), 0)
    firsts = range(0, onehot_ref.shape[0], tree)
    parents = [parents_ref[first:first + tree, :] - first for first in firsts]
    jumps = [(parent == lanes).astype(BF16) for parent in parents]
    depths = [jnp.broadcast_to((parent != rows).astype(F32), (tree, 128)) for parent in parents]
    for level in range((tree - 1).bit_length()):
        depths = [
            depth + jnp.dot(jump, depth.astype(BF16), preferred_element_type=F32)
            for depth, jump in zip(depths, jumps)
        ]
        jumps = [jnp.dot(jump, jump, preferred_element_type=F32).astype(BF16) for jump in jumps]
    for first, depth in zip(firsts, depths):
        onehot_ref[first:first + tree, :] = (depth[:, :1].astype(jnp.int32) == lanes).astype(BF16)


def depth_onehot(parents, tree):
    rows = parents.shape[0]
    return pl.pallas_call(
        functools.partial(onehot_kernel, tree),
        name="onehot",
        out_shape=jax.ShapeDtypeStruct((rows, tree), BF16),
        compiler_params=params(16),
        cost_estimate=cost(48 * rows * tree * tree, 8 * rows * tree),
    )(parents[:, None])


def forward_kernel(place_ref, near_ref, far_ref, *refs):
    out_ref = refs[-1]
    outer = jnp.logical_or(place_ref[1] == 0, place_ref[1] == 3)

    @pl.when(outer)
    def _():
        out_ref[...] = near_ref[...]

    @pl.when(jnp.logical_not(outer))
    def _():
        out_ref[...] = far_ref[...]


def forward(place, near, far, after, long):
    return pl.pallas_call(
        forward_kernel,
        name="forward",
        out_shape=jax.ShapeDtypeStruct(near.shape, near.dtype),
        in_specs=[SMEM, VMEM, VMEM] + [ANY] * len(after),
        out_specs=VMEM,
        compiler_params=params(8),
        cost_estimate=cost(0, 6 * near.size, long),
    )(place, near, far, *after)


def slot_of(dest, chips, gx):
    ahead = lax.rem(dest // 2 - gx // 2 + 2 * chips - 1, chips)
    return jnp.where(lax.rem(gx, 2) == lax.rem(dest, 2), chips, 0) + ahead


def look_kernel(count, chips, block, first, exclusive, place_ref, onehot_ref, table_ref, *refs):
    looked_ref = refs[-1]
    size = looked_ref.shape[0] // count
    for dest in range(count):
        here = pl.ds(dest * block + first, size)
        looked = jnp.dot(onehot_ref[here, :], table_ref[...], preferred_element_type=F32)
        slot = pl.multiple_of(slot_of(dest, chips, place_ref[0]) * size, 16)
        looked_ref[pl.ds(slot, size), :] = looked.astype(BF16)


def look(chips, count, block, first, size, exclusive, place, onehot, table, after):
    depth = table.shape[1]
    tile = divisor(depth, (896, 512, 256, 128))
    return pl.pallas_call(
        functools.partial(look_kernel, count, chips, block, first, exclusive),
        name="look",
        grid=(depth // tile,),
        out_shape=jax.ShapeDtypeStruct((count * size, depth), BF16),
        in_specs=[SMEM, pl.BlockSpec(onehot.shape, lambda j: (0, 0)), pl.BlockSpec((table.shape[0], tile), lambda j: (0, j))]
        + [ANY] * len(after),
        out_specs=pl.BlockSpec((count * size, tile), lambda j: (0, j)),
        compiler_params=params(16),
        cost_estimate=cost(2 * count * size * table.shape[0] * depth, 4 * count * size * depth),
    )(place, onehot, table, *after)


def arrange_kernel(count, chips, exclusive, added, place_ref, *refs):
    rows_ref = refs[-1]
    size = rows_ref.shape[0] // count
    for held in range(count):
        dest = lax.bitwise_xor(place_ref[1], held) if exclusive else held
        here = pl.ds(pl.multiple_of(slot_of(dest, chips, place_ref[0]) * size, 16), size)
        if added:
            rows_ref[here, :] = (refs[held][...].astype(F32) + refs[count][here, :].astype(F32)).astype(BF16)
        else:
            rows_ref[here, :] = refs[held][...]


def arrange(chips, exclusive, place, held, looked, after):
    count = len(held)
    size, depth = held[0].shape
    added = [] if looked is None else [looked]
    return pl.pallas_call(
        functools.partial(arrange_kernel, count, chips, exclusive, bool(added)),
        name="arrange",
        out_shape=jax.ShapeDtypeStruct((count * size, depth), BF16),
        in_specs=[SMEM] + [VMEM] * (count + len(added)) + [ANY] * len(after),
        out_specs=VMEM,
        compiler_params=params(16),
        cost_estimate=cost(count * size * depth, 6 * count * size * depth),
    )(place, *held, *added, *after)


def embed_own_kernel(block, first, place_ref, onehot_ref, table_ref, hidden_ref, *refs):
    start = place_ref[1] * block
    for rows_ref in refs:
        size = rows_ref.shape[0]
        here = pl.ds(pl.multiple_of(start + first, 16), size)
        looked = jnp.dot(onehot_ref[here, :], table_ref[...], preferred_element_type=F32)
        rows_ref[...] = (hidden_ref[first:first + size, :].astype(F32) + looked).astype(BF16)
        first += size


def embed_own(sizes, place, onehot, table, hidden):
    block, depth = hidden.shape
    tile = divisor(depth, (896, 512, 256, 128))
    column = lambda j: (0, j)
    return pl.pallas_call(
        functools.partial(embed_own_kernel, block, block - sum(sizes)),
        name="own",
        grid=(depth // tile,),
        out_shape=[jax.ShapeDtypeStruct((size, depth), BF16) for size in sizes],
        in_specs=[
            SMEM,
            pl.BlockSpec(onehot.shape, lambda j: (0, 0)),
            pl.BlockSpec((table.shape[0], tile), column),
            pl.BlockSpec((block, tile), column),
        ],
        out_specs=[pl.BlockSpec((size, tile), column) for size in sizes],
        compiler_params=params(16),
        cost_estimate=cost(2 * sum(sizes) * table.shape[0] * depth, 6 * sum(sizes) * depth),
    )(place, onehot, table, hidden)


def gelu_sum(terms):
    total = terms[0].astype(F32)
    for term in terms[1:]:
        total = total + term.astype(F32)
    return jax.nn.gelu(total, approximate=True).astype(BF16)


def product_kernel(start, tile, steps, slots, ending, rows_ref, lead_ref, weight_ref, *refs):
    terms = refs[:ending[3]]
    outs = 2 if not ending[3] else 3
    scratch = len(refs) - (2 if not ending[3] else 6)
    send_ref, keep_ref = refs[scratch - outs:scratch - outs + 2]
    held, arrived = refs[scratch:scratch + 2]
    half = send_ref.shape[0]
    step = pl.program_id(0)

    def fetch(index):
        column = pl.multiple_of(start + index * tile, 128)
        slot = lax.rem(index, slots)
        return pltpu.make_async_copy(weight_ref.at[:, pl.ds(column, tile)], held.at[slot], arrived.at[slot])

    if ending[3]:
        out_ref = refs[scratch - 1]
        term_buffer, out_buffer, term_sems, out_sem = refs[scratch + 2:]
        row, column, width, number = ending
        given = [pltpu.make_async_copy(terms[n], term_buffer.at[n], term_sems.at[n]) for n in range(number)]
        place_out = out_ref.at[row:row + out_buffer.shape[0], column:column + width]
        taken = pltpu.make_async_copy(out_buffer, place_out, out_sem.at[0])

    @pl.when(step == 0)
    def _():
        for index in range(1, min(slots - 1, steps)):
            fetch(index).start()
        if ending[3]:
            for copy in given:
                copy.start()

    @pl.when(step + slots - 1 < steps)
    def _():
        fetch(step + slots - 1).start()

    def multiply(tile_ref):
        out = jnp.dot(rows_ref[...], tile_ref[...], preferred_element_type=F32)
        send_ref[...] = out[:half].astype(BF16)
        keep_ref[...] = out[half:].astype(BF16)

    @pl.when(step == 0)
    def _():
        multiply(lead_ref)

    @pl.when(step > 0)
    def _():
        fetch(step).wait()
        multiply(held.at[lax.rem(step, slots)])

    if ending[3]:
        @pl.when(step == 0)
        def _():
            for copy in given:
                copy.wait()
            part = divisor(width, (512, 384, 256, 128))

            @pl.loop(0, width // part)
            def _(index):
                here = pl.ds(pl.multiple_of(index * part, 128), part)
                out_buffer[:, here] = gelu_sum([term_buffer[n, :, here] for n in range(number)])

            taken.start()

        @pl.when(step == steps - 1)
        def _():
            taken.wait()


def tile_of(width):
    return divisor(width, (512, 384, 256, 128))


def product(rows, lead, weight, start, width, after, ending=None, terms=(), out=None, shape=None):
    height, depth = rows.shape
    tile = lead.shape[1]
    slots = 4
    half = jax.ShapeDtypeStruct((height // 2, width), BF16)
    outs = [half, half]
    out_specs = [pl.BlockSpec((height // 2, tile), lambda j: (0, j))] * 2
    scratch = [
        pltpu.VMEM((slots, depth, tile), BF16),
        pltpu.SemaphoreType.DMA((slots,)),
    ]
    operands = [rows, lead, weight, *terms]
    aliases = {}
    ending = (0, 0, 0, 0) if not terms else (*ending, terms[0].shape[1], len(terms))
    if terms:
        outs.append(jax.ShapeDtypeStruct(shape, BF16))
        out_specs.append(ANY)
        scratch += [
            pltpu.VMEM((len(terms), *terms[0].shape), BF16),
            pltpu.VMEM(terms[0].shape, BF16),
            pltpu.SemaphoreType.DMA((len(terms),)),
            pltpu.SemaphoreType.DMA((1,)),
        ]
        if out is not None:
            aliases = {len(operands): 2}
            operands.append(out)
    operands += after
    return pl.pallas_call(
        functools.partial(product_kernel, start, tile, width // tile, slots, ending),
        name="product",
        grid=(width // tile,),
        out_shape=outs,
        in_specs=[VMEM] * 2 + [ANY] * (len(operands) - 2),
        out_specs=out_specs,
        scratch_shapes=scratch,
        input_output_aliases=aliases,
        compiler_params=params(24),
        cost_estimate=cost(2 * height * depth * width, 2 * (height * depth + depth * width + height * width)),
    )(*operands)


def pair_kernel(keep_ref, got_ref, *refs):
    away_ref, stay_ref = refs[-2:]
    cut = away_ref.shape[0]
    total = keep_ref[...].astype(F32) + got_ref[...].astype(F32)
    away_ref[...] = total[:cut].astype(BF16)
    stay_ref[...] = total[cut:].astype(BF16)


def pair(chips, keep, got, after, long):
    height, width = keep.shape
    size = height // chips
    tile = width // 2 if width % 256 == 0 else width
    spec = lambda rows: pl.BlockSpec((rows, tile), lambda j: (0, j))
    return pl.pallas_call(
        pair_kernel,
        name="pair",
        grid=(width // tile,),
        out_shape=[jax.ShapeDtypeStruct((height - size, width), BF16), jax.ShapeDtypeStruct((size, width), BF16)],
        in_specs=[spec(height), spec(height)] + [ANY] * len(after),
        out_specs=[spec(height - size), spec(size)],
        compiler_params=params(16),
        cost_estimate=cost(height * width, 6 * height * width, long),
    )(keep, got, *after)


def finish_kernel(count, *refs):
    out_ref, token_ref = refs[-2:]
    out_ref[...] = gelu_sum([refs[index][...] for index in range(count)])
    token_ref[...] = jnp.zeros_like(token_ref)


def finish(shape, step, rows, terms, held, after, long):
    index, start, width = step
    tile = divisor(width, (1536, 1152, 768, 512, 384, 256, 128))
    aliases = {} if held is None else {len(terms): 0}
    return pl.pallas_call(
        functools.partial(finish_kernel, len(terms)),
        name="finish",
        grid=(width // tile,),
        out_shape=[jax.ShapeDtypeStruct(shape, BF16), jax.ShapeDtypeStruct((8, 128), F32)],
        in_specs=[pl.BlockSpec((rows, tile), lambda j: (0, j))] * len(terms) + [ANY] * (len(aliases) + len(after)),
        out_specs=[
            pl.BlockSpec((rows, tile), lambda j: (index, start // tile + j)),
            pl.BlockSpec((8, 128), lambda j: (0, 0)),
        ],
        input_output_aliases=aliases,
        compiler_params=params(16),
        cost_estimate=cost(12 * rows * width, 6 * rows * width, long),
    )(*terms, *([] if held is None else [held]), *after)


def column_pieces(columns, shares):
    unit, start, pieces = columns // sum(shares), 0, []
    for share in shares:
        pieces.append((start, share * unit))
        start += share * unit
    return pieces


SHARES = ((10, 8), (6, 6, 6), (6, 6, 6))


def chunk_sizes(block):
    if block % 192 == 0:
        return [block // 3, block * 5 // 12, block // 4]
    return [block // 3] * 3


ORDER = (
    ("f0", "a0", "p00", "f1", "p01", "s00"),
    ("a1", "t2", "p10", "s01", "p11-00", "f2", "s10", "p12-01", "s11"),
    ("a2", "p20-10", "s12", "p21-11", "s20", "p22-12+", "g20!"),
    ("s21!", "s22", "g21", "g22"),
)


def local(n_gx, n_gy, hidden, parents, depth_table, weight):
    tree = depth_table.shape[0]
    columns = weight.shape[1]
    block = hidden.shape[0]
    chips = n_gx // 2
    sizes = chunk_sizes(block)
    firsts = [sum(sizes[:index]) for index in range(len(sizes))]
    parts = len(sizes)
    place = jnp.stack([lax.axis_index("gx"), lax.axis_index("gy")]).astype(jnp.int32)

    exclusive = n_gy == 4

    def swap(array, distance):
        return lax.ppermute(array, "gy", [(k, k ^ distance) for k in range(n_gy)])

    def later(array, token):
        return lax.optimization_barrier((array, token))[0]

    def take(index, token):
        if not exclusive:
            whole = lax.all_gather(own[index], "gy", axis=0)
            held[index] = [whole[k] for k in range(n_gy)]
        else:
            rows = own[index] if token is None else later(own[index], token)
            held[index] = [own[index], None if index == 1 else swap(rows, 1), swap(rows, 2)]

    own, held = [hidden[:sizes[0]]], [None] * parts
    take(0, None)
    onehot = depth_onehot(parents, tree)
    own += embed_own(sizes[1:], place, onehot, depth_table, hidden)

    sibling = [(g, g ^ 1) for g in range(n_gx)]

    def across(ahead):
        return [(g, (g // 2 + ahead) % chips * 2 + g % 2) for g in range(n_gx)]

    out, after = None, own[1:2]
    pieces = [column_pieces(columns, shares) for shares in SHARES]
    products, sums, waiting = {}, {}, {}
    for item in sum(ORDER, ()):
        long = item.endswith("!")
        late = item.endswith("+")
        item = item.rstrip("!+")
        kind, index, piece = item[0], int(item[1]), item[1:3]
        if kind == "f":
            if exclusive:
                given = forward(place, held[index][1], held[index][2], after, long)
                held[index].append(lax.ppermute(given, "gy", [(0, 2), (1, 0), (2, 3), (3, 1)]))
                after = [given]
            if index == 0:
                take(1, after[0] if after else None)
                looked = look(chips, n_gx, block, 0, sizes[0], exclusive, place, onehot, depth_table, after)
                cuts = sorted({(start, tile_of(width)) for each in pieces for start, width in each})
                ready = later(weight, looked)
                if exclusive:
                    held[1][1] = swap(later(own[1], looked), 1)
                leads = {(start, tile): ready[:, start:start + tile] for start, tile in cuts}
        if kind == "t":
            take(index, after[0])
        if kind == "a":
            rows = arrange(chips, exclusive, place, held[index], None if index else looked, after)
            after = [rows]
        if kind == "p":
            start, width = pieces[index][int(item[2])]
            extra = {}
            if len(item) > 3:
                done = item[4:]
                ending = (firsts[int(done[0])], pieces[int(done[0])][int(done[1])][0])
                extra = dict(ending=ending, terms=sums[done], out=out, shape=(block, columns))
            send, keep, *rest = product(rows, leads[start, tile_of(width)], weight, start, width, after, **extra)
            out = rest[0] if rest else out
            after = [keep]
            if late:
                waiting[piece] = keep, send
            else:
                products[piece] = keep, lax.ppermute(send, "gx", sibling)
        if kind == "s":
            away, stay = pair(chips, *products[piece], after, long)
            size = sizes[index]
            sums[piece] = [stay] + [
                lax.ppermute(away[(ahead - 1) * size:ahead * size], "gx", across(ahead)) for ahead in range(1, chips)
            ]
            after = [stay]
        if kind == "g":
            start, width = pieces[index][int(item[2])]
            out, token = finish((block, columns), (firsts[index] // sizes[index], start, width), sizes[index], sums[piece], out, after, long)
            after = [token]
            for name, (keep, send) in waiting.items():
                products[name] = keep, lax.ppermute(later(send, token), "gx", sibling)
            waiting = {}
    return out


def solution(mesh):
    return jax.shard_map(
        functools.partial(local, mesh.shape["gx"], mesh.shape["gy"]),
        mesh=mesh,
        in_specs=(P(("grp", "gy"), "gx"), P("grp"), P(None, "gx"), P("gx", "gy")),
        out_specs=P(("grp", "gx"), "gy"),
        check_vma=False,
    )
```
